512 devices in a mesh: lon: 32 (over z_lo, x), lat: 16 (over y, z_hi, core).
Axes of the slice: x: 4, y: 4, z: 16 (z_hi: 2, z_lo: 8; z = z_hi * 8 + z_lo), core: 2. Of those that a mesh axis runs over, the one named last changes fastest.
Arguments:
- fields: bfloat16 [128, 1024, 256], P('lat', 'lon'), may hold values from -6 to 6
- cotangent: bfloat16 [128, 1024, 256], P('lat', 'lon'), may hold values from -6 to 6
- land_sea: int32 [128, 1024], P('lat', 'lon'), may hold values 0 or 1
- partner: int32 [1024], replicated, may hold values from 0 to 1023, as said below
- kernel: float32 [7, 7, 256], replicated, may hold values from -0.875 to 0.875
- gain: float32 [256], replicated, may hold values from 0.25 to 1.75
- w_in: bfloat16 [1024, 256], replicated, may hold values from -0.375 to 0.375
- w_out: bfloat16 [1024, 256], replicated, may hold values from -0.1875 to 0.1875
Outputs:
- block_out: bfloat16 [128, 1024, 256], P('lat', 'lon')
- grad_input: bfloat16 [128, 1024, 256], P('lat', 'lon')
- grad_w_in: float32 [1024, 256], P(('lon', 'lat'))
- grad_w_out: float32 [1024, 256], P(('lon', 'lat'))
- grad_kernel: float32 [7, 7, 256], replicated
- grad_gain: float32 [256], replicated
The draws below stay inside these ranges and needn't reach their ends.
Inputs may be any that keep to these rules, and one draw needn't show every extreme that they name: partner[i] = (s - i) mod 1024 for one s per draw, so the table is its own inverse.
All inputs are finite; a program needn't handle non-finite values. No bound on the sum of `land_sea` on one device may be relied on, other than what follows from the above.
Results may differ from the reference program's by a relative error of at most 0.0055.
Values may be sent and summed in bfloat16 or wider, within the bound.
No kernel may reach another device: no remote copies, remote signals or barrier semaphores. Data moves between devices by JAX's collectives and lax.ppermute only.
A program may use at most 64 MiB of HBM per device.

```python
import jax
import jax.numpy as jnp
from jax import lax

C = 256
FF = 1024
KERNEL = 7
LAT_DEV = 8
NLAT = 128
NLON = 1024


def draw_partner(key, part):
    key = jax.random.fold_in(key, 11)
    numbers = jax.random.randint(key, (NLON,), 0, NLON, dtype=jnp.int32)
    offset = (jnp.sum(numbers % NLON) % NLON).astype(jnp.int32)
    columns = jnp.arange(NLON, dtype=jnp.int32)
    return ((offset - columns) % NLON).astype(jnp.int32)


def set_ends(values, key, least, top_value):
    shape = values.shape
    place = [jax.random.randint(jax.random.fold_in(key, axis), (), 0, shape[axis]) for axis in range(len(shape))]
    values = values.at[tuple(place)].set(least)
    longest = shape.index(max(shape))
    place[longest] = (place[longest] + 1) % shape[longest]
    return values.at[tuple(place)].set(top_value)


def block_levels(own_key, extent, cuts, smallest, largest):
    factor_of = 1.0
    for dim, shards_of in cuts:
        draws = jax.random.uniform(jax.random.fold_in(jax.random.fold_in(own_key, 6), dim), (shards_of,), jnp.float32, smallest / len(cuts), largest / len(cuts))
        factor_of = factor_of * jnp.repeat(jnp.exp(draws), extent[dim] // shards_of).reshape((-1,) + (1,) * (len(extent) - 1 - dim))
    return factor_of


def bell_draw(rng, extent, scale, most, cuts=(), kind=jnp.bfloat16):
    loudness = block_levels(rng, extent, cuts, -0.22, 0.18) if cuts else 1.0
    values = jax.random.normal(rng, extent, jnp.float32) * scale * loudness
    return jnp.minimum(jnp.maximum(values, -most), most).astype(kind)


def setup_inputs(seed: int = 0) -> dict:
    streams_of = jax.random.split(jax.random.key(seed), 9)
    return {
        "fields": bell_draw(streams_of[0], (NLAT, NLON, C), 1.0, 6.0, ((0, 16), (1, 32))),
        "cotangent": bell_draw(streams_of[1], (NLAT, NLON, C), 1.0, 6.0, ((0, 16), (1, 32))),
        "land_sea": set_ends((jax.random.randint(streams_of[2], (NLAT, NLON), 0, 4) < 3).astype(jnp.int32), jax.random.fold_in(streams_of[2], 1), 0, 1),
        "partner": draw_partner(jax.random.fold_in(streams_of[8], 71), 0),
        "kernel": bell_draw(streams_of[4], (KERNEL, KERNEL, C), (KERNEL * KERNEL) ** -0.5, 0.875, (), jnp.float32),
        "gain": jnp.clip(1.0 + 0.15 * jax.random.normal(streams_of[5], (C,), jnp.float32), 0.25, 1.75),
        "w_in": bell_draw(streams_of[6], (FF, C), C ** -0.5, 0.375),
        "w_out": bell_draw(streams_of[7], (FF, C), FF ** -0.5, 0.1875),
    }


EPS = 1e-06

def gelu_slope(values):
    result, pullback = jax.vjp(lambda inner: jax.nn.gelu(inner, approximate=True), values)
    return pullback(jnp.ones_like(values))[0]

def reference(fields, cotangent, land_sea, partner, kernel, gain, w_in, w_out):
    width = fields.shape[2]
    source = fields.astype(jnp.float32)
    upper = source[::-1][:3][:, partner]
    padded = jnp.concatenate([jnp.zeros((3, NLON, width), jnp.float32), source, upper], 0)
    padded = jnp.concatenate([padded[:, NLON - 3:], padded, padded[:, :3]], 1)
    conved = jnp.zeros((NLAT, NLON, width), jnp.float32)
    for row_tap in range(7):
        for col_tap in range(7):
            conved = conved + padded[row_tap:row_tap + NLAT, col_tap:col_tap + NLON] * kernel[row_tap, col_tap]
    count = LAT_DEV * NLON
    blocks = NLAT // LAT_DEV

    def split(array):
        return array.reshape((blocks, count) + array.shape[2:])
    keep_all = land_sea.astype(jnp.float32)

    def step(carry, pieces):
        grad_in, grad_out, grad_gain = carry
        conv_rows, field_rows, cot_rows, mask_rows = pieces
        average = lax.optimization_barrier(jnp.mean(conv_rows, -1, keepdims=True))
        centred = conv_rows - average
        rstd = lax.rsqrt(lax.optimization_barrier(jnp.mean(centred * centred, -1, keepdims=True)) + EPS)
        normed = centred * rstd
        scaled = (normed * gain).astype(jnp.bfloat16)
        before = jnp.dot(scaled, w_in.T, preferred_element_type=jnp.float32)
        hidden = jax.nn.gelu(before, approximate=True).astype(jnp.bfloat16)
        branch = jnp.dot(hidden, w_out, preferred_element_type=jnp.float32)
        keeper = mask_rows[:, None]
        result = (keeper * (field_rows.astype(jnp.float32) + branch)).astype(jnp.bfloat16)
        upstream = keeper * cot_rows.astype(jnp.float32)
        upstream_b = upstream.astype(jnp.bfloat16)
        grad_out = grad_out + jnp.dot(hidden.T, upstream_b, preferred_element_type=jnp.float32)
        dhidden = jnp.dot(upstream_b, w_out.T, preferred_element_type=jnp.float32)
        dbefore = (dhidden * gelu_slope(before)).astype(jnp.bfloat16)
        grad_in = grad_in + jnp.dot(dbefore.T, scaled, preferred_element_type=jnp.float32)
        dscaled = jnp.dot(dbefore, w_in, preferred_element_type=jnp.float32)
        grad_gain = grad_gain + lax.optimization_barrier(jnp.sum(dscaled * normed, 0))
        dnormed = dscaled * gain
        dconved = rstd * (dnormed - lax.optimization_barrier(jnp.mean(dnormed, -1, keepdims=True)) - normed * lax.optimization_barrier(jnp.mean(dnormed * normed, -1, keepdims=True)))
        return ((grad_in, grad_out, grad_gain), (result, dconved, upstream))
    start = (jnp.zeros((w_in.shape[0], width), jnp.float32), jnp.zeros((w_in.shape[0], width), jnp.float32), jnp.zeros((width,), jnp.float32))
    sums, outputs = lax.scan(step, start, (split(conved), split(fields), split(cotangent), split(keep_all)))
    block_out = outputs[0].reshape(NLAT, NLON, width)
    dconved = outputs[1].reshape(NLAT, NLON, width)
    upstream = outputs[2].reshape(NLAT, NLON, width)
    kernel_terms = []
    dpadded = jnp.zeros((NLAT + 6, NLON + 6, width), jnp.float32)
    for row_tap in range(7):
        for col_tap in range(7):
            kernel_terms.append(lax.optimization_barrier(jnp.sum(padded[row_tap:row_tap + NLAT, col_tap:col_tap + NLON] * dconved, (0, 1))))
            dpadded = dpadded.at[row_tap:row_tap + NLAT, col_tap:col_tap + NLON].add(kernel[row_tap, col_tap] * dconved)
    core = dpadded[:, 3:NLON + 3]
    core = core.at[:, :3].add(dpadded[:, NLON + 3:])
    core = core.at[:, NLON - 3:].add(dpadded[:, :3])
    inner = core[3:NLAT + 3]
    upper_rim = core[NLAT + 3:]
    inner = inner.at[NLAT - 3:].add(upper_rim[:, partner][::-1])
    grad_input = (upstream + inner).astype(jnp.bfloat16)
    factor = float(NLAT * NLON) ** (-0.5)
    grad_kernel = jnp.stack(kernel_terms).reshape(7, 7, width) * factor
    return (block_out, grad_input, sums[0] * factor, sums[1] * factor, grad_kernel, sums[2] * factor)
```

```python
import functools
import math

import jax
import jax.numpy as jnp
from jax import lax
from jax.experimental import pallas as pl
from jax.experimental.pallas import tpu as pltpu
from jax.sharding import PartitionSpec as P

EPS = 1e-06
ROWS, COLS, WIDTH, HIDDEN = 8, 32, 256, 1024
CELLS = ROWS * COLS
LANES = 128
CHUNK = 256
LEFT = 8
SMALL = 64
FOLD = 4
GELU_A = math.sqrt(2.0 / math.pi)
GELU_B = 0.044715
STAGES = ((0,), (3, 2), (5, 4), (1, 8), (7, 6))
SPLIT_STAGE = 2

f32, bf16 = jnp.float32, jnp.bfloat16


def dot(left, right, dims):
    return lax.dot_general(left, right, (dims, ((), ())), preferred_element_type=f32)


def packed(value):
    high = value.astype(bf16)
    low = (value - high.astype(f32)).astype(bf16)
    return high, low


def unpacked(high, low):
    return high.astype(f32) + low.astype(f32)


def assemble(info, own, south, north, west, east, folds, wide, fold):
    wide[pl.ds(3, ROWS), pl.ds(LEFT, COLS), :] = own[...].astype(f32)
    wide[pl.ds(0, 3), pl.ds(LEFT, COLS), :] = south[...].astype(f32)
    wide[:, pl.ds(LEFT - 3, 3), :] = west[...].astype(f32)
    wide[:, pl.ds(LEFT + COLS, 3), :] = east[...].astype(f32)

    @pl.when(info[0] == 0)
    def _():
        wide[pl.ds(ROWS + 3, 3), pl.ds(LEFT, COLS), :] = north[...].astype(f32)

    @pl.when(info[0] == 1)
    def _():
        for place, part in enumerate(folds):
            fold[:, pl.ds(place * COLS, COLS), :] = part[...].astype(f32)
        for column in range(COLS + 6):
            source = 2 * COLS + info[1] - column
            for row in range(3):
                wide[ROWS + 3 + row, pl.ds(LEFT - 3 + column, 1), :] = fold[2 - row, pl.ds(source, 1), :]


def main_kernel(
    info, own, south, north, west, east, fold0, fold1, fold2, cot, land, taps, gain, w_in, w_out,
    block_out, dconv, keep, message, sums, wide, fold, grid,
):
    assemble(info, own, south, north, west, east, (fold0, fold1, fold2), wide, fold)
    for half in range(WIDTH // LANES):
        lanes = pl.ds(half * LANES, LANES)
        for tile in range(COLS // 8):
            total = jnp.zeros((ROWS, 8, LANES), f32)
            for b in range(7):
                block = wide[:, pl.ds(LEFT - 3 + tile * 8 + b, 8), lanes]
                for a in range(7):
                    total = total + block[a : a + ROWS] * taps[pl.ds(7 * a + b, 1), lanes][None]
            grid[:, pl.ds(tile * 8, 8), lanes] = total
    flat = grid[...].reshape(CELLS, WIDTH)
    average = jnp.mean(flat, -1, keepdims=True)
    centred = flat - average
    rstd = lax.rsqrt(jnp.mean(centred * centred, -1, keepdims=True) + EPS)
    normed = centred * rstd
    gains = gain[...]
    scaled = (normed * gains).astype(bf16)
    keeper = land[...].astype(f32)
    upstream = (keeper * cot[...].reshape(CELLS, WIDTH).astype(f32)).astype(bf16)
    branch = jnp.zeros((CELLS, WIDTH), f32)
    dscaled = jnp.zeros((CELLS, WIDTH), f32)
    for part in range(2):
        for chunk in range(HIDDEN // 2 // CHUNK):
            start = pl.multiple_of((info[2] ^ part) * (HIDDEN // 2) + chunk * CHUNK, CHUNK)
            w_in_part, w_out_part = w_in[pl.ds(start, CHUNK), :], w_out[pl.ds(start, CHUNK), :]
            before = dot(scaled, w_in_part, ((1,), (1,)))
            square = before * before
            bend = jnp.tanh(before * (GELU_A + (GELU_A * GELU_B) * square))
            gate = 0.5 + 0.5 * bend
            hidden = (before * gate).astype(bf16)
            slope = gate + (0.5 * before) * (1.0 - bend * bend) * (GELU_A + (3.0 * GELU_A * GELU_B) * square)
            branch = branch + dot(hidden, w_out_part, ((1,), (0,)))
            dbefore = (dot(upstream, w_out_part, ((1,), (1,))) * slope).astype(bf16)
            dscaled = dscaled + dot(dbefore, w_in_part, ((1,), (0,)))
            target = message if part else keep
            units = pl.ds(chunk * CHUNK + SMALL * part, CHUNK)
            target[units, pl.ds(0, WIDTH)] = dot(dbefore, scaled, ((0,), (0,))).astype(target.dtype)
            target[units, pl.ds(WIDTH, WIDTH)] = dot(hidden, upstream, ((0,), (0,))).astype(target.dtype)
    centre = own[...].reshape(CELLS, WIDTH).astype(f32)
    block_out[...] = (keeper * (centre + branch)).astype(bf16).reshape(ROWS, COLS, WIDTH)
    dnormed = dscaled * gains
    dconved = rstd * (
        dnormed - jnp.mean(dnormed, -1, keepdims=True) - normed * jnp.mean(dnormed * normed, -1, keepdims=True)
    )
    dconv[...] = dconved.astype(bf16).reshape(ROWS, COLS, WIDTH)
    grid[...] = dconved.reshape(ROWS, COLS, WIDTH)
    sums[pl.ds(48, 16), :] = jnp.zeros((16, WIDTH), f32)
    sums[pl.ds(49, 1), :] = jnp.sum(dscaled * normed, 0, keepdims=True)
    for half in range(WIDTH // LANES):
        lanes = pl.ds(half * LANES, LANES)
        for b in range(7):
            totals = [jnp.zeros((8, LANES), f32) for _ in range(7)]
            for tile in range(COLS // 8):
                block = wide[:, pl.ds(LEFT - 3 + tile * 8 + b, 8), lanes]
                here = grid[:, pl.ds(tile * 8, 8), lanes]
                for a in range(7):
                    totals[a] = totals[a] + jnp.sum(block[a : a + ROWS] * here, 0)
            for a in range(7):
                sums[pl.ds(7 * a + b, 1), lanes] = jnp.sum(totals[a], 0, keepdims=True)
    high, low = packed(sums[...])
    message[pl.ds(0, SMALL), pl.ds(0, WIDTH)] = high
    message[pl.ds(0, SMALL), pl.ds(WIDTH, WIDTH)] = low
    sums[...] = unpacked(high, low)


def grad_input_kernel(
    info, own, south, north, west, east, fold0, fold1, fold2, cot, land, taps, grad_input, wide, fold, upstream
):
    assemble(info, own, south, north, west, east, (fold0, fold1, fold2), wide, fold)
    folded = info[0] == 1
    masked = land[...].astype(f32) * cot[...].reshape(CELLS, WIDTH).astype(f32)
    upstream[...] = masked.reshape(ROWS, COLS, WIDTH)
    for half in range(WIDTH // LANES):
        lanes = pl.ds(half * LANES, LANES)
        for tile in range(COLS // 8):
            total = upstream[:, pl.ds(tile * 8, 8), lanes]
            for b in range(7):
                block = wide[:, pl.ds(LEFT - 3 + tile * 8 + b, 8), lanes]
                for a in range(7):
                    weight = taps[pl.ds(48 - (7 * a + b), 1), lanes][None]
                    if a > 3:
                        rim = jnp.where(folded, taps[pl.ds(7 * a + b, 1), lanes][None], weight)
                        weight = jnp.concatenate(
                            [
                                jnp.broadcast_to(weight, (11 - a, 1, LANES)),
                                jnp.broadcast_to(rim, (a - 3, 1, LANES)),
                            ],
                            0,
                        )
                    total = total + block[a : a + ROWS] * weight
            grid_part = total.astype(bf16)
            grad_input[:, pl.ds(tile * 8, 8), lanes] = grid_part


def pairwise(parts):
    while len(parts) > 1:
        parts = [left + right for left, right in zip(parts[::2], parts[1::2])]
    return parts[0]


def padded(span):
    return max(span, 16)


def combined(rows, keep, sums, received):
    large, small = pl.ds(sums.shape[0], padded(rows)), pl.ds(0, sums.shape[0])
    total = pairwise([keep[...]] + [part[large, :].astype(f32)[:rows] for part in received])
    others = [unpacked(part[small, pl.ds(0, WIDTH)], part[small, pl.ds(WIDTH, WIDTH)]) for part in received]
    return total, pairwise([sums[...]] + others)


def stage_kernel(have, want, split, index, keep, sums, *refs):
    received, messages = refs[: have - 1], refs[have - 1 : have - 1 + want - 1]
    keep_out, sums_out, stack, small = refs[have - 1 + want - 1 :]
    rows = keep.shape[0]
    span = rows // want
    total, total_sums = combined(rows, keep, sums, received)
    height = sums_out.shape[0]
    for part in range(want):
        stack[part] = total[part * span : part * span + span]
    high, low = packed(total_sums)
    if split:
        both = jnp.concatenate([high.astype(f32), low.astype(f32)], 1)
        for part in range(want):
            small[part] = both[part * height : part * height + height]
    for mask in range(1, want):
        message = messages[mask - 1]
        large = stack[index[0] ^ mask]
        if span < padded(span):
            large = jnp.concatenate([large, jnp.zeros((padded(span) - span, 2 * WIDTH), f32)], 0)
        message[pl.ds(height, padded(span)), :] = large.astype(bf16)
        if split:
            message[pl.ds(0, height), :] = small[index[0] ^ mask].astype(bf16)
        else:
            message[pl.ds(0, height), pl.ds(0, WIDTH)] = high
            message[pl.ds(0, height), pl.ds(WIDTH, WIDTH)] = low
    keep_out[...] = stack[index[0]]
    if split:
        mine = small[index[0]]
        sums_out[...] = mine[:, :WIDTH] + mine[:, WIDTH:]
    else:
        sums_out[...] = unpacked(high, low)


def last_kernel(factor, have, keep, sums, *refs):
    received, (first, second, small) = refs[: have - 1], refs[have - 1 :]
    total, total_sums = combined(keep.shape[0], keep, sums, received)
    first[...] = total[:, :WIDTH] * factor
    second[...] = total[:, WIDTH:] * factor
    small[...] = total_sums * factor


def gather_kernel(index, own, *refs):
    others, (grad_kernel, grad_gain, stack) = refs[:-3], refs[-3:]
    height = own.shape[0]
    for mask, part in enumerate((own,) + others):
        place = pl.multiple_of((index[0] ^ mask) * height, height)
        stack[pl.ds(place, height), :] = part[...]
    for row in range(7):
        grad_kernel[row] = stack[pl.ds(7 * row, 7), :]
    grad_gain[...] = stack[pl.ds(49, 1), :]


def run(kernel, out, scratch, scalars, *args):
    whole = pl.BlockSpec(memory_space=pltpu.VMEM)
    specs = [pl.BlockSpec(memory_space=pltpu.SMEM)] * (scalars is not None) + [whole] * len(args)
    call = pl.pallas_call(
        kernel,
        out_shape=out,
        in_specs=specs,
        out_specs=jax.tree.map(lambda _: whole, out),
        scratch_shapes=scratch,
        compiler_params=pltpu.CompilerParams(vmem_limit_bytes=48 * 1024 * 1024),
    )
    return call(*(() if scalars is None else (scalars,)), *args)


def fold_reflect(step, lat_count, lon_count):
    pairs = [
        (((step - lon) % lon_count + 1) * lat_count - 1, (lon + 1) * lat_count - 1) for lon in range(lon_count)
    ]
    return lambda last: lax.ppermute(last, ("lon", "lat"), pairs)


def fold_rotate(step, lat_count, lon_count):
    def moved(value, offset):
        if offset == 0:
            return value
        pairs = [
            (((lon + offset) % lon_count + 1) * lat_count - 1, (lon + 1) * lat_count - 1) for lon in range(lon_count)
        ]
        return lax.ppermute(value, ("lon", "lat"), pairs)

    return lambda value: tuple(moved(value, offset - step) for offset in (2, 1, 0))


def halo(value, shift):
    rows, cols, width = value.shape
    lat_count, lon_count = lax.axis_size("lat"), lax.axis_size("lon")
    first, last = value[:3], value[rows - 3 :]
    block = shift // cols
    south = lax.ppermute(last, "lat", [(i, i + 1) for i in range(lat_count - 1)])
    north = lax.ppermute(first, "lat", [(i + 1, i) for i in range(lat_count - 1)])
    reflected = lax.switch(
        block // FOLD, [fold_reflect(FOLD * k, lat_count, lon_count) for k in range(lon_count // FOLD)], last
    )
    ring = [(i, (i + 1) % lon_count) for i in range(lon_count)]
    right = jnp.concatenate([south[:, cols - 3 :], value[:, cols - 3 :], north[:, cols - 3 :]], 0)
    left = jnp.concatenate([south[:, :3], value[:, :3], north[:, :3]], 0)
    west = lax.ppermute(right, "lon", ring)
    east = lax.ppermute(left, "lon", [(j, i) for i, j in ring])
    folds = lax.switch(block % FOLD, [fold_rotate(k, lat_count, lon_count) for k in range(FOLD)], reflected)
    return (value, south, north, west, east) + tuple(folds)


def exchange(bits, messages):
    count = lax.axis_size("lat") * lax.axis_size("lon")
    out = []
    for mask, message in enumerate(messages, 1):
        flips = sum(1 << bit for place, bit in enumerate(reversed(bits)) if mask >> place & 1)
        out.append(lax.ppermute(message, ("lon", "lat"), [(i, i ^ flips) for i in range(count)]))
    return out


def stage_index(bits):
    flat = lax.axis_index("lon") * lax.axis_size("lat") + lax.axis_index("lat")
    index = 0
    for bit in bits:
        index = 2 * index + (flat >> bit & 1)
    return index


def reordered(weights):
    count = sum(len(bits) for bits in STAGES)
    order = [count - 1 - bit for bits in STAGES for bit in bits]
    split = weights.reshape((2,) * count + (weights.shape[0] >> count, weights.shape[1]))
    return split.transpose(order + [count, count + 1]).reshape(weights.shape)


def body(fields, cotangent, land_sea, partner, kernel, gain, w_in, w_out):
    shape = jax.ShapeDtypeStruct
    total_cols = COLS * lax.axis_size("lon")
    shift = (partner[0] + 3) % total_cols
    at_top = lax.axis_index("lat") == lax.axis_size("lat") - 1
    info = jnp.stack([at_top.astype(jnp.int32), shift % COLS, stage_index(STAGES[0])])
    taps = kernel.reshape(49, WIDTH)
    land = land_sea.reshape(CELLS, 1)
    grid_shape = shape((ROWS, COLS, WIDTH), bf16)
    wide = pltpu.VMEM((ROWS + 6, COLS + 16, WIDTH), f32)
    fold = pltpu.VMEM((3, 3 * COLS, WIDTH), f32)
    grid = pltpu.VMEM((ROWS, COLS, WIDTH), f32)
    rows = HIDDEN // 2
    block_out, dconved, keep, message, sums = run(
        main_kernel,
        (
            grid_shape,
            grid_shape,
            shape((rows, 2 * WIDTH), f32),
            shape((rows + SMALL, 2 * WIDTH), bf16),
            shape((SMALL, WIDTH), f32),
        ),
        [wide, fold, grid],
        info,
        *halo(fields, shift),
        cotangent,
        land,
        taps,
        gain.reshape(1, WIDTH),
        reordered(w_in),
        reordered(w_out),
    )
    messages = [message]
    height = SMALL
    for stage in range(len(STAGES) - 1):
        received = exchange(STAGES[stage], messages)
        want, split = 1 << len(STAGES[stage + 1]), stage + 1 == SPLIT_STAGE
        span = rows // want
        height = height // want if split else height
        *messages, keep, sums = run(
            functools.partial(stage_kernel, len(received) + 1, want, split),
            tuple([shape((padded(span) + height, 2 * WIDTH), bf16)] * (want - 1))
            + (shape((span, 2 * WIDTH), f32), shape((height, WIDTH), f32)),
            [pltpu.VMEM((want, span, 2 * WIDTH), f32), pltpu.VMEM((want, height, 2 * WIDTH), f32)],
            stage_index(STAGES[stage + 1]).reshape(1),
            keep,
            sums,
            *received,
        )
        rows = span
    received = exchange(STAGES[-1], messages)
    factor = 1.0 / math.sqrt(CELLS * lax.axis_size("lat") * lax.axis_size("lon"))
    share = shape((rows, WIDTH), f32)
    grad_w_in, grad_w_out, small = run(
        functools.partial(last_kernel, factor, len(received) + 1),
        (share, share, shape((height, WIDTH), f32)),
        [],
        None,
        keep,
        sums,
        *received,
    )
    bits = STAGES[SPLIT_STAGE]
    grad_kernel, grad_gain = run(
        gather_kernel,
        (shape((7, 7, WIDTH), f32), shape((1, WIDTH), f32)),
        [pltpu.VMEM((SMALL, WIDTH), f32)],
        stage_index(bits).reshape(1),
        small,
        *exchange(bits, [small] * ((1 << len(bits)) - 1)),
    )
    grad_input = run(
        grad_input_kernel, grid_shape, [wide, fold, grid], info, *halo(dconved, shift), cotangent, land, taps
    )
    return block_out, grad_input, grad_w_in, grad_w_out, grad_kernel, grad_gain.reshape(WIDTH)


def solution(mesh):
    cells = P("lat", "lon", None)
    share = P(("lon", "lat"), None)
    return jax.shard_map(
        body,
        mesh=mesh,
        in_specs=(cells, cells, P("lat", "lon"), P(), P(), P(), P(), P()),
        out_specs=(cells, cells, share, share, P(), P()),
        check_vma=False,
    )
```

```python
import functools
import math

import jax
import jax.numpy as jnp
import numpy as np
from jax import lax
from jax.experimental import pallas as pl
from jax.experimental.pallas import tpu as pltpu
from jax.sharding import PartitionSpec as P

EPS = 1e-06
ROWS, COLS, WIDTH, HIDDEN = 8, 32, 256, 1024
CELLS = ROWS * COLS
LANES = 128
CHUNK = 256
LEFT = 8
ACROSS = 4
EDGE = 8
SPAN = COLS + EDGE
FOLD = 2
BEYOND = 5
GELU_A = math.sqrt(2.0 / math.pi)
GELU_B = 0.044715
f32, bf16 = jnp.float32, jnp.bfloat16


def dot(left, right, dims):
    return lax.dot_general(left, right, (dims, ((), ())), preferred_element_type=f32)


def edges(info, grid, messages):
    block = grid[ROWS - 3 :].reshape(3 * COLS, WIDTH).astype(bf16)
    left, right = [
        grid[:, start : start + EDGE].reshape(ROWS * EDGE, WIDTH).astype(bf16) for start in (0, COLS - EDGE)
    ]
    even = info[1] == 0
    for message, here, there in zip(messages, (right, left), (left, right)):
        message[pl.ds(0, ROWS * EDGE), :] = jnp.where(even, here.astype(f32), there.astype(f32)).astype(bf16)
        message[pl.ds(ROWS * EDGE, 3 * COLS), :] = block


def edge_kernel(info, own, *messages):
    edges(info, own[...].astype(f32), messages)


def middle(info, wide, first, own, sides):
    wide[pl.ds(first, ROWS), pl.ds(LEFT, COLS), :] = own[...].astype(f32)
    margin = pl.ds(0, ROWS * EDGE)
    for parity, starts in enumerate(((LEFT + COLS, 0), (0, LEFT + COLS))):

        @pl.when(info[1] == parity)
        def _():
            for start, side in zip(starts, sides):
                part = side[margin, :].astype(f32).reshape(ROWS, EDGE, WIDTH)
                wide[pl.ds(first, ROWS), pl.ds(start, EDGE), :] = part


def rows_kernel(info, turn, own, side0, side1, *refs):
    near, far, window, extra, wide, line = refs[-6:]
    middle(info, wide, 0, own, (side0, side1))
    columns = pl.ds(LEFT - 3, SPAN)
    for parity, order in enumerate(((near, far), (far, near))):

        @pl.when(info[2] == parity)
        def _():
            for message, start in zip(order, (ROWS - 3, 0)):
                message[...] = wide[pl.ds(start, 3), columns, :].reshape(3 * SPAN, WIDTH).astype(bf16)

    @pl.when(info[0] == 1)
    def _():
        block = pl.ds(ROWS * EDGE, 3 * COLS)
        line[:, pl.ds(COLS, COLS), :] = own[pl.ds(ROWS - 3, 3)].astype(f32)
        for parity, starts in enumerate(((2 * COLS, 0), (0, 2 * COLS))):

            @pl.when(info[1] == parity)
            def _():
                for start, side in zip(starts, (side0, side1)):
                    line[:, pl.ds(start, COLS), :] = side[block, :].astype(f32).reshape(3, COLS, WIDTH)

        for column in range(COLS + 6):
            source = jnp.maximum(COLS + turn[0] - column, 0)
            for row in range(3):
                wide[row, pl.ds(column, 1), :] = line[2 - row, pl.ds(source, 1), :]
            if column > COLS:
                source = jnp.minimum((FOLD + 1) * COLS + turn[0] - column, 3 * COLS - 1)
                for row in range(3):
                    wide[3 + row, pl.ds(column - COLS - 1, 1), :] = line[2 - row, pl.ds(source, 1), :]
        extra[pl.ds(0, 3 * EDGE), :] = wide[pl.ds(3, 3), pl.ds(0, EDGE), :].reshape(3 * EDGE, WIDTH).astype(bf16)
        window[...] = wide[pl.ds(0, 3), pl.ds(0, SPAN), :].reshape(3 * SPAN, WIDTH).astype(bf16)


def assemble(info, turn, own, side0, side1, near, far, window, extra, wide):
    middle(info, wide, 3, own, (side0, side1))
    columns = pl.ds(LEFT - 3, SPAN)
    for parity, (below, above) in enumerate(((far, near), (near, far))):

        @pl.when(info[2] == parity)
        def _():
            for part, start in ((below, 0), (above, ROWS + 3)):
                wide[pl.ds(start, 3), columns, :] = part[...].astype(f32).reshape(3, SPAN, WIDTH)

    @pl.when(info[0] == 1)
    def _():
        wide[pl.ds(ROWS + 3, 3), columns, :] = window[...].astype(f32).reshape(3, SPAN, WIDTH)
        rest = extra[pl.ds(0, 3 * EDGE), :].astype(f32).reshape(3, EDGE, WIDTH)
        for place in range(BEYOND):
            column = COLS + 1 + place

            @pl.when(turn[0] - column < -COLS)
            def _():
                wide[pl.ds(ROWS + 3, 3), pl.ds(LEFT - 3 + column, 1), :] = rest[:, place : place + 1]


def keepers(land):
    spot = lax.broadcasted_iota(jnp.int32, (1, COLS, COLS), 1) == lax.broadcasted_iota(jnp.int32, (1, COLS, COLS), 2)
    values = land[...].astype(f32)[:, None, :]
    return jnp.sum(jnp.where(spot, values, 0.0), -1, keepdims=True)


def main_kernel(
    info, turn, own, side0, side1, near, far, window, extra, cot, land, taps, gain, w_in, w_out,
    block_out, dconv, message0, message1, message, wide, grid, sums,
):
    assemble(info, turn, own, side0, side1, near, far, window, extra, wide)
    for half in range(WIDTH // LANES):
        lanes = pl.ds(half * LANES, LANES)
        for tile in range(COLS // 8):
            total = jnp.zeros((ROWS, 8, LANES), f32)
            for b in range(7):
                block = wide[:, pl.ds(LEFT - 3 + tile * 8 + b, 8), lanes]
                for a in range(7):
                    total = total + block[a : a + ROWS] * taps[a, pl.ds(b, 1), lanes][None]
            grid[:, pl.ds(tile * 8, 8), lanes] = total
    flat = grid[...].reshape(CELLS, WIDTH)
    average = jnp.mean(flat, -1, keepdims=True)
    centred = flat - average
    rstd = lax.rsqrt(jnp.mean(centred * centred, -1, keepdims=True) + EPS)
    normed = centred * rstd
    gains = gain[...]
    scaled = (normed * gains).astype(bf16)
    keeper = keepers(land)
    upstream = (keeper * cot[...].astype(f32)).astype(bf16).reshape(CELLS, WIDTH)
    branch = jnp.zeros((CELLS, WIDTH), f32)
    dscaled = jnp.zeros((CELLS, WIDTH), f32)
    plane, span = message.shape[0], HIDDEN // message.shape[0]
    for chunk in range(HIDDEN // CHUNK):
        units = pl.ds(chunk * CHUNK, CHUNK)
        w_in_part, w_out_part = w_in[units, :], w_out[units, :]
        before = dot(scaled, w_in_part, ((1,), (1,)))
        square = before * before
        bend = jnp.tanh(before * (GELU_A + (GELU_A * GELU_B) * square))
        gate = 0.5 + 0.5 * bend
        hidden = (before * gate).astype(bf16)
        slope = gate + (0.5 * before) * (1.0 - bend * bend) * (GELU_A + (3.0 * GELU_A * GELU_B) * square)
        branch = branch + dot(hidden, w_out_part, ((1,), (0,)))
        dbefore = (dot(upstream, w_out_part, ((1,), (1,))) * slope).astype(bf16)
        dscaled = dscaled + dot(dbefore, w_in_part, ((1,), (0,)))
        places = pl.ds(chunk * CHUNK // span, CHUNK // span)
        for pair, (units_of, cells_of) in enumerate(((dbefore, scaled), (hidden, upstream))):
            product = dot(units_of, cells_of, ((0,), (0,))).astype(bf16)
            for half in range(2):
                part = product[:, half * LANES : half * LANES + LANES]
                message[places, pl.ds((2 * pair + half) * span, span), :] = part.reshape(CHUNK // span, span, LANES)
    block_out[...] = (keeper * (own[...].astype(f32) + branch.reshape(ROWS, COLS, WIDTH))).astype(bf16)
    dnormed = dscaled * gains
    dconved = rstd * (
        dnormed - jnp.mean(dnormed, -1, keepdims=True) - normed * jnp.mean(dnormed * normed, -1, keepdims=True)
    )
    dconv[...] = dconved.astype(bf16).reshape(ROWS, COLS, WIDTH)
    grid[...] = dconved.reshape(ROWS, COLS, WIDTH)
    edges(info, grid[...], (message0, message1))
    gain_row = jnp.sum(dscaled * normed, 0, keepdims=True)
    sums[...] = jnp.zeros(sums.shape, f32)
    for half in range(WIDTH // LANES):
        lanes = pl.ds(half * LANES, LANES)
        sums[49 // 2, pl.ds(2 + half, 1), :] = gain_row[:, half * LANES : half * LANES + LANES]
        for b in range(7):
            totals = [jnp.zeros((8, LANES), f32) for _ in range(7)]
            for tile in range(COLS // 8):
                block = wide[:, pl.ds(LEFT - 3 + tile * 8 + b, 8), lanes]
                here = grid[:, pl.ds(tile * 8, 8), lanes]
                for a in range(7):
                    totals[a] = totals[a] + jnp.sum(block[a : a + ROWS] * here, 0)
            for a in range(7):
                tap = 7 * a + b
                sums[tap // 2, pl.ds(2 * (tap % 2) + half, 1), :] = jnp.sum(totals[a], 0, keepdims=True)
    message[:, pl.ds(4 * span, 16), :] = small_pack(sums[...]).astype(bf16)


def small_pack(sums):
    high = sums.astype(bf16).astype(f32)
    low = sums - high
    return jnp.concatenate([high[:, :4], low[:, :4], jnp.zeros_like(sums)], 1)


def grad_input_kernel(
    info, turn, own, side0, side1, near, far, window, extra, cot, land, taps, grad_input, wide, upstream
):
    assemble(info, turn, own, side0, side1, near, far, window, extra, wide)
    folded = info[0] == 1
    upstream[...] = keepers(land) * cot[...].astype(f32)
    for half in range(WIDTH // LANES):
        lanes = pl.ds(half * LANES, LANES)
        for tile in range(COLS // 8):
            total = upstream[:, pl.ds(tile * 8, 8), lanes]
            for b in range(7):
                block = wide[:, pl.ds(LEFT - 3 + tile * 8 + b, 8), lanes]
                for a in range(7):
                    weight = taps[6 - a, pl.ds(6 - b, 1), lanes][None]
                    if a > 3:
                        rim = jnp.where(folded, taps[a, pl.ds(b, 1), lanes][None], weight)
                        weight = jnp.concatenate(
                            [
                                jnp.broadcast_to(weight, (11 - a, 1, LANES)),
                                jnp.broadcast_to(rim, (a - 3, 1, LANES)),
                            ],
                            0,
                        )
                    total = total + block[a : a + ROWS] * weight
            grid_part = total.astype(bf16)
            grad_input[:, pl.ds(tile * 8, 8), lanes] = grid_part


def plane_kernel(received, *refs):
    message, total = refs[-2:]
    plane, lines = received.shape[0], received.shape[1] - 16
    depth = message.shape[0]
    each = lines // 4 // depth
    large = received[0, pl.ds(0, lines), :].astype(f32)
    small = received[0, pl.ds(lines, 16), :].astype(f32)
    for source in range(1, plane):
        large = large + received[source, pl.ds(0, lines), :].astype(f32)
        small = small + received[source, pl.ds(lines, 16), :].astype(f32)
    total[...] = large
    sums = small[:8]
    both = sums + jnp.concatenate([sums[4:], sums[:4]], 0)
    packed = small_pack(both[None])[0, :8]
    for place in range(depth):
        parts = [total[pl.ds(line * (lines // 4) + place * each, each), :] for line in range(4)]
        message[place] = jnp.concatenate(parts + [packed], 0).astype(bf16)


def depth_kernel(factor, received, *refs):
    first, second, message = refs[-3:]
    depth, lines = received.shape[0], received.shape[1] - 8
    total = received[0].astype(f32)
    for source in range(1, depth):
        total = total + received[source].astype(f32)
    total = total * factor
    each = lines // 4
    for half in range(2):
        lanes = pl.ds(half * LANES, LANES)
        first[:, lanes] = total[half * each : half * each + each]
        second[:, lanes] = total[(2 + half) * each : (3 + half) * each]
    sums = total[lines:]
    both = sums + jnp.concatenate([sums[4:], sums[:4]], 0)
    message[...] = jnp.broadcast_to(both[None], message.shape)


def gather_kernel(received, grad_kernel, grad_gain):
    for tap in range(50):
        for half in range(WIDTH // LANES):
            lanes = pl.ds(half * LANES, LANES)
            row = received[tap // 2, pl.ds(2 * (tap % 2) + half, 1), :]
            if tap == 49:
                grad_gain[:, lanes] = row
            else:
                grad_kernel[tap // 7, pl.ds(tap % 7, 1), lanes] = row


def run(kernel, out, scratch, scalars, *args, waits=()):
    whole = pl.BlockSpec(memory_space=pltpu.VMEM)
    specs = [pl.BlockSpec(memory_space=pltpu.SMEM)] * len(scalars) + [whole] * len(args)
    specs += [pl.BlockSpec(memory_space=pl.ANY)] * len(waits)
    call = pl.pallas_call(
        kernel,
        out_shape=out,
        in_specs=specs,
        out_specs=jax.tree.map(lambda _: whole, out),
        scratch_shapes=scratch,
        compiler_params=pltpu.CompilerParams(vmem_limit_bytes=48 * 1024 * 1024),
    )
    return call(*scalars, *args, *waits)


def swapped(value, axis, start, wrap):
    count = lax.axis_size(axis)
    pairs = [(i, (i + 1) % count) for i in range(start, count if wrap else count - 1, 2)]
    return lax.ppermute(value, axis, pairs + [(j, i) for i, j in pairs])


def fold_stage(step, lat_count, lon_count):
    pairs = [
        (((step - lon) % lon_count + 1) * lat_count - 1, (lon + 1) * lat_count - 1) for lon in range(lon_count)
    ]
    return lambda value: lax.ppermute(value, ("lon", "lat"), pairs)


def halo(info, turn, value, messages, shift, waits=()):
    sides = [swapped(message, "lon", start, True) for start, message in enumerate(messages)]
    rows = jax.ShapeDtypeStruct((3 * SPAN, WIDTH), bf16)
    near, far, window, extra = run(
        rows_kernel,
        (rows, rows, rows, jax.ShapeDtypeStruct((4 * EDGE, WIDTH), bf16)),
        [pltpu.VMEM((ROWS, COLS + 16, WIDTH), f32), pltpu.VMEM((3, 3 * COLS, WIDTH), f32)],
        (info, turn),
        value,
        *sides,
        waits=waits,
    )
    far = swapped(far, "lat", 1, False)
    near = swapped(near, "lat", 0, False)
    lat_count, lon_count = lax.axis_size("lat"), lax.axis_size("lon")
    moves = [fold_stage(FOLD * k, lat_count, lon_count) for k in range(lon_count // FOLD)]

    def branch(k, whole):
        return lambda window, extra: (moves[k](window), extra if whole else moves[k - 1](extra))

    branches = [branch(k, whole) for k in range(len(moves)) for whole in (True, False)]
    chosen = 2 * (shift // (FOLD * COLS)) + (turn[0] < BEYOND)
    return value, *sides, near, far, *lax.switch(chosen, branches, window, extra)


def layout():
    lat_count, lon_count = lax.axis_size("lat"), lax.axis_size("lon")
    high = 2 if lat_count > 2 else 1
    return (lon_count // ACROSS, ACROSS, lat_count // (2 * high), high, 2)


def device_groups():
    numbers = np.arange(math.prod(layout())).reshape(layout()).transpose(4, 2, 1, 3, 0)
    plane = math.prod(numbers.shape[:3])
    lines = numbers.reshape(plane, -1)
    return lines.T.tolist(), lines.tolist()


def spread(value, groups):
    return lax.all_to_all(value, ("lon", "lat"), 0, 0, axis_index_groups=groups, tiled=True)


def reordered(weights):
    split = weights.reshape(layout() + (-1, weights.shape[1]))
    return split.transpose(4, 2, 1, 3, 0, 5, 6).reshape(weights.shape)


def body(fields, cotangent, land_sea, partner, kernel, gain, w_in, w_out):
    shape = jax.ShapeDtypeStruct
    total_cols = COLS * lax.axis_size("lon")
    shift = (partner[0] + 3) % total_cols
    turn = (shift % (FOLD * COLS)).reshape(1)
    at_top = lax.axis_index("lat") == lax.axis_size("lat") - 1
    info = jnp.stack([at_top.astype(jnp.int32), lax.axis_index("lon") % 2, lax.axis_index("lat") % 2])
    grid_shape = shape((ROWS, COLS, WIDTH), bf16)
    side = shape((ROWS * EDGE + 3 * COLS, WIDTH), bf16)
    edge_shapes = (side, side)
    wide = pltpu.VMEM((ROWS + 6, COLS + 16, WIDTH), f32)
    grid = pltpu.VMEM((ROWS, COLS, WIDTH), f32)
    planes, lines = device_groups()
    plane, depth = len(planes[0]), len(lines[0])
    span = HIDDEN // plane
    weights = reordered(w_in), reordered(w_out)
    sent = run(edge_kernel, edge_shapes, [], (info,), fields)
    block_out, dconved, message0, message1, message = run(
        main_kernel,
        (grid_shape, grid_shape) + edge_shapes + (shape((plane, 4 * span + 16, LANES), bf16),),
        [wide, grid, pltpu.VMEM((plane, 8, LANES), f32)],
        (info, turn),
        *halo(info, turn, fields, sent, shift, weights),
        cotangent,
        land_sea,
        kernel,
        gain.reshape(1, WIDTH),
        *weights,
    )
    rims = halo(info, turn, dconved, (message0, message1), shift)
    message = run(
        plane_kernel,
        shape((depth, 4 * span // depth + 8, LANES), bf16),
        [pltpu.VMEM((4 * span, LANES), f32)],
        (),
        spread(message, planes),
        waits=rims[1:3],
    )
    factor = 1.0 / math.sqrt(CELLS * lax.axis_size("lat") * lax.axis_size("lon"))
    share = shape((span // depth, WIDTH), f32)
    grad_w_in, grad_w_out, message = run(
        functools.partial(depth_kernel, factor),
        (share, share, shape((plane, 8, LANES), f32)),
        [],
        (),
        spread(message, lines),
        waits=rims[3:],
    )
    grad_kernel, grad_gain = run(
        gather_kernel,
        (shape((7, 7, WIDTH), f32), shape((1, WIDTH), f32)),
        [],
        (),
        spread(message, planes),
    )
    grad_input = run(grad_input_kernel, grid_shape, [wide, grid], (info, turn), *rims, cotangent, land_sea, kernel)
    return block_out, grad_input, grad_w_in, grad_w_out, grad_kernel, grad_gain.reshape(WIDTH)


def solution(mesh):
    cells = P("lat", "lon", None)
    share = P(("lon", "lat"), None)
    return jax.shard_map(
        body,
        mesh=mesh,
        in_specs=(cells, cells, P("lat", "lon"), P(), P(), P(), P(), P()),
        out_specs=(cells, cells, share, share, P(), P()),
        check_vma=False,
    )
```

```python
import functools
import math

import jax
import jax.numpy as jnp
import numpy as np
from jax import lax
from jax.experimental import pallas as pl
from jax.experimental.pallas import tpu as pltpu
from jax.sharding import PartitionSpec as P

EPS = 1e-06
ROWS, COLS, WIDTH, HIDDEN = 8, 32, 256, 1024
CELLS = ROWS * COLS
LANES = 128
CHUNK = 256
LEFT = 8
ACROSS = 4
EDGE = 8
SPAN = COLS + EDGE
FOLD = 2
BEYOND = 5
GELU_A = math.sqrt(2.0 / math.pi)
GELU_B = 0.044715
f32, bf16 = jnp.float32, jnp.bfloat16


def dot(left, right, dims):
    return lax.dot_general(left, right, (dims, ((), ())), preferred_element_type=f32)


def put(wide, rows, columns, value):
    for half in range(WIDTH // LANES):
        wide[half, rows, columns, :] = value[..., half * LANES : half * LANES + LANES]


def edges(info, grid, messages):
    block = grid[ROWS - 3 :].reshape(3 * COLS, WIDTH).astype(bf16)
    left, right = [
        grid[:, start : start + EDGE].reshape(ROWS * EDGE, WIDTH).astype(bf16) for start in (0, COLS - EDGE)
    ]
    even = info[1] == 0
    for message, here, there in zip(messages, (right, left), (left, right)):
        message[pl.ds(0, ROWS * EDGE), :] = jnp.where(even, here.astype(f32), there.astype(f32)).astype(bf16)
        message[pl.ds(ROWS * EDGE, 3 * COLS), :] = block


def edge_kernel(info, own, *messages):
    edges(info, own[...].astype(f32), messages)


def middle(info, wide, first, own, sides):
    put(wide, pl.ds(first, ROWS), pl.ds(LEFT, COLS), own[...].astype(f32))
    margin = pl.ds(0, ROWS * EDGE)
    for parity, starts in enumerate(((LEFT + COLS, 0), (0, LEFT + COLS))):

        @pl.when(info[1] == parity)
        def _():
            for start, side in zip(starts, sides):
                part = side[margin, :].astype(f32).reshape(ROWS, EDGE, WIDTH)
                put(wide, pl.ds(first, ROWS), pl.ds(start, EDGE), part)


def rows_kernel(info, turn, own, side1, side0, *refs):
    near, far, window, extra, wide, line, strip = refs[-7:]
    middle(info, wide, 0, own, (side0, side1))
    columns = pl.ds(LEFT - 3, SPAN)
    for parity, order in enumerate(((near, far), (far, near))):

        @pl.when(info[2] == parity)
        def _():
            for message, start in zip(order, (ROWS - 3, 0)):
                for half in range(WIDTH // LANES):
                    part = wide[half, pl.ds(start, 3), columns, :].reshape(3 * SPAN, LANES)
                    message[:, pl.ds(half * LANES, LANES)] = part.astype(bf16)

    @pl.when(info[0] == 1)
    def _():
        block = pl.ds(ROWS * EDGE, 3 * COLS)
        line[:, pl.ds(COLS, COLS), :] = own[pl.ds(ROWS - 3, 3)].astype(f32)
        for parity, starts in enumerate(((2 * COLS, 0), (0, 2 * COLS))):

            @pl.when(info[1] == parity)
            def _():
                for start, side in zip(starts, (side0, side1)):
                    line[:, pl.ds(start, COLS), :] = side[block, :].astype(f32).reshape(3, COLS, WIDTH)

        for column in range(COLS + 6):
            source = jnp.maximum(COLS + turn[0] - column, 0)
            for row in range(3):
                strip[row, pl.ds(column, 1), :] = line[2 - row, pl.ds(source, 1), :]
            if column > COLS:
                source = jnp.minimum((FOLD + 1) * COLS + turn[0] - column, 3 * COLS - 1)
                for row in range(3):
                    strip[3 + row, pl.ds(column - COLS - 1, 1), :] = line[2 - row, pl.ds(source, 1), :]
        extra[pl.ds(0, 3 * EDGE), :] = strip[pl.ds(3, 3), pl.ds(0, EDGE), :].reshape(3 * EDGE, WIDTH).astype(bf16)
        window[...] = strip[pl.ds(0, 3), :, :].reshape(3 * SPAN, WIDTH).astype(bf16)


def assemble(info, turn, own, side1, side0, far, near, window, extra, wide):
    middle(info, wide, 3, own, (side0, side1))
    columns = pl.ds(LEFT - 3, SPAN)
    for parity, (below, above) in enumerate(((far, near), (near, far))):

        @pl.when(info[2] == parity)
        def _():
            for part, start in ((below, 0), (above, ROWS + 3)):
                put(wide, pl.ds(start, 3), columns, part[...].astype(f32).reshape(3, SPAN, WIDTH))

    @pl.when(info[0] == 1)
    def _():
        put(wide, pl.ds(ROWS + 3, 3), columns, window[...].astype(f32).reshape(3, SPAN, WIDTH))
        rest = extra[pl.ds(0, 3 * EDGE), :].astype(f32).reshape(3, EDGE, WIDTH)
        for place in range(BEYOND):
            column = COLS + 1 + place

            @pl.when(turn[0] - column < -COLS)
            def _():
                put(wide, pl.ds(ROWS + 3, 3), pl.ds(LEFT - 3 + column, 1), rest[:, place : place + 1])


def keepers(land):
    spot = lax.broadcasted_iota(jnp.int32, (1, COLS, COLS), 1) == lax.broadcasted_iota(jnp.int32, (1, COLS, COLS), 2)
    values = land[...].astype(f32)[:, None, :]
    return jnp.sum(jnp.where(spot, values, 0.0), -1, keepdims=True)


def main_kernel(
    info, turn, own, side1, side0, far, near, window, extra, cot, land, taps, gain, w_in, w_out,
    block_out, dconv, message0, message1, message, wide, grid, sums,
):
    assemble(info, turn, own, side1, side0, far, near, window, extra, wide)
    for half in range(WIDTH // LANES):
        lanes = pl.ds(half * LANES, LANES)
        for tile in range(COLS // 8):
            total = jnp.zeros((ROWS, 8, LANES), f32)
            for b in range(7):
                block = wide[half, :, pl.ds(LEFT - 3 + tile * 8 + b, 8), :]
                for a in range(7):
                    total = total + block[a : a + ROWS] * taps[a, pl.ds(b, 1), lanes][None]
            grid[:, pl.ds(tile * 8, 8), lanes] = total
    flat = grid[...].reshape(CELLS, WIDTH)
    average = jnp.mean(flat, -1, keepdims=True)
    centred = flat - average
    rstd = lax.rsqrt(jnp.mean(centred * centred, -1, keepdims=True) + EPS)
    normed = centred * rstd
    gains = gain[...]
    scaled = (normed * gains).astype(bf16)
    keeper = keepers(land)
    upstream = (keeper * cot[...].astype(f32)).astype(bf16).reshape(CELLS, WIDTH)
    branch = jnp.zeros((CELLS, WIDTH), f32)
    dscaled = jnp.zeros((CELLS, WIDTH), f32)
    plane, span = message.shape[0], HIDDEN // message.shape[0]
    for chunk in range(HIDDEN // CHUNK):
        units = pl.ds(chunk * CHUNK, CHUNK)
        w_in_part, w_out_part = w_in[units, :], w_out[units, :]
        before = dot(scaled, w_in_part, ((1,), (1,)))
        square = before * before
        bend = jnp.tanh(before * (GELU_A + (GELU_A * GELU_B) * square))
        gate = 0.5 + 0.5 * bend
        hidden = (before * gate).astype(bf16)
        slope = gate + (0.5 * before) * (1.0 - bend * bend) * (GELU_A + (3.0 * GELU_A * GELU_B) * square)
        branch = branch + dot(hidden, w_out_part, ((1,), (0,)))
        dbefore = (dot(upstream, w_out_part, ((1,), (1,))) * slope).astype(bf16)
        dscaled = dscaled + dot(dbefore, w_in_part, ((1,), (0,)))
        places = pl.ds(chunk * CHUNK // span, CHUNK // span)
        for pair, (units_of, cells_of) in enumerate(((dbefore, scaled), (hidden, upstream))):
            product = dot(units_of, cells_of, ((0,), (0,))).astype(bf16)
            for half in range(2):
                part = product[:, half * LANES : half * LANES + LANES]
                message[places, pl.ds((2 * pair + half) * span, span), :] = part.reshape(CHUNK // span, span, LANES)
    block_out[...] = (keeper * (own[...].astype(f32) + branch.reshape(ROWS, COLS, WIDTH))).astype(bf16)
    dnormed = dscaled * gains
    dconved = rstd * (
        dnormed - jnp.mean(dnormed, -1, keepdims=True) - normed * jnp.mean(dnormed * normed, -1, keepdims=True)
    )
    dconv[...] = dconved.astype(bf16).reshape(ROWS, COLS, WIDTH)
    grid[...] = dconved.reshape(ROWS, COLS, WIDTH)
    edges(info, grid[...], (message0, message1))
    gain_row = jnp.sum(dscaled * normed, 0, keepdims=True)
    sums[...] = jnp.zeros(sums.shape, f32)
    for half in range(WIDTH // LANES):
        lanes = pl.ds(half * LANES, LANES)
        sums[49 // 2, pl.ds(2 + half, 1), :] = gain_row[:, half * LANES : half * LANES + LANES]
        for b in range(7):
            totals = [jnp.zeros((8, LANES), f32) for _ in range(7)]
            for tile in range(COLS // 8):
                block = wide[half, :, pl.ds(LEFT - 3 + tile * 8 + b, 8), :]
                here = grid[:, pl.ds(tile * 8, 8), lanes]
                for a in range(7):
                    totals[a] = totals[a] + jnp.sum(block[a : a + ROWS] * here, 0)
            for a in range(7):
                tap = 7 * a + b
                sums[tap // 2, pl.ds(2 * (tap % 2) + half, 1), :] = jnp.sum(totals[a], 0, keepdims=True)
    message[:, pl.ds(4 * span, 16), :] = small_pack(sums[...]).astype(bf16)


def small_pack(sums):
    high = sums.astype(bf16).astype(f32)
    low = sums - high
    return jnp.concatenate([high[:, :4], low[:, :4], jnp.zeros_like(sums)], 1)


def grad_input_kernel(
    info, turn, own, side1, side0, far, near, window, extra, cot, land, taps, grad_input, wide, upstream
):
    assemble(info, turn, own, side1, side0, far, near, window, extra, wide)
    folded = info[0] == 1
    upstream[...] = keepers(land) * cot[...].astype(f32)
    for half in range(WIDTH // LANES):
        lanes = pl.ds(half * LANES, LANES)
        for tile in range(COLS // 8):
            total = upstream[:, pl.ds(tile * 8, 8), lanes]
            for b in range(7):
                block = wide[half, :, pl.ds(LEFT - 3 + tile * 8 + b, 8), :]
                for a in range(7):
                    weight = taps[6 - a, pl.ds(6 - b, 1), lanes][None]
                    if a > 3:
                        rim = jnp.where(folded, taps[a, pl.ds(b, 1), lanes][None], weight)
                        weight = jnp.concatenate(
                            [
                                jnp.broadcast_to(weight, (11 - a, 1, LANES)),
                                jnp.broadcast_to(rim, (a - 3, 1, LANES)),
                            ],
                            0,
                        )
                    total = total + block[a : a + ROWS] * weight
            grid_part = total.astype(bf16)
            grad_input[:, pl.ds(tile * 8, 8), lanes] = grid_part


def plane_kernel(received, *refs):
    message, total = refs[-2:]
    plane, lines = received.shape[0], received.shape[1] - 16
    depth = message.shape[0]
    each = lines // 4 // depth
    large = received[0, pl.ds(0, lines), :].astype(f32)
    small = received[0, pl.ds(lines, 16), :].astype(f32)
    for source in range(1, plane):
        large = large + received[source, pl.ds(0, lines), :].astype(f32)
        small = small + received[source, pl.ds(lines, 16), :].astype(f32)
    total[...] = large
    sums = small[:8]
    both = sums + jnp.concatenate([sums[4:], sums[:4]], 0)
    packed = small_pack(both[None])[0, :8]
    for place in range(depth):
        parts = [total[pl.ds(line * (lines // 4) + place * each, each), :] for line in range(4)]
        message[place] = jnp.concatenate(parts + [packed], 0).astype(bf16)


def depth_kernel(factor, received, *refs):
    first, second, message = refs[-3:]
    depth, lines = received.shape[0], received.shape[1] - 8
    total = received[0].astype(f32)
    for source in range(1, depth):
        total = total + received[source].astype(f32)
    total = total * factor
    each = lines // 4
    for half in range(2):
        lanes = pl.ds(half * LANES, LANES)
        first[:, lanes] = total[half * each : half * each + each]
        second[:, lanes] = total[(2 + half) * each : (3 + half) * each]
    sums = total[lines:]
    both = sums + jnp.concatenate([sums[4:], sums[:4]], 0)
    message[...] = jnp.broadcast_to(both[None], message.shape)


def gather_kernel(received, grad_kernel, grad_gain):
    for tap in range(50):
        for half in range(WIDTH // LANES):
            lanes = pl.ds(half * LANES, LANES)
            row = received[tap // 2, pl.ds(2 * (tap % 2) + half, 1), :]
            if tap == 49:
                grad_gain[:, lanes] = row
            else:
                grad_kernel[tap // 7, pl.ds(tap % 7, 1), lanes] = row


def run(kernel, out, scratch, scalars, *args, waits=()):
    whole = pl.BlockSpec(memory_space=pltpu.VMEM)
    specs = [pl.BlockSpec(memory_space=pltpu.SMEM)] * len(scalars) + [whole] * len(args)
    specs += [pl.BlockSpec(memory_space=pl.ANY)] * len(waits)
    call = pl.pallas_call(
        kernel,
        out_shape=out,
        in_specs=specs,
        out_specs=jax.tree.map(lambda _: whole, out),
        scratch_shapes=scratch,
        compiler_params=pltpu.CompilerParams(vmem_limit_bytes=48 * 1024 * 1024),
    )
    return call(*scalars, *args, *waits)


def swapped(value, axis, start, wrap):
    count = lax.axis_size(axis)
    pairs = [(i, (i + 1) % count) for i in range(start, count if wrap else count - 1, 2)]
    return lax.ppermute(value, axis, pairs + [(j, i) for i, j in pairs])


def fold_stage(step, lat_count, lon_count):
    pairs = [
        (((step - lon) % lon_count + 1) * lat_count - 1, (lon + 1) * lat_count - 1) for lon in range(lon_count)
    ]
    return lambda value: lax.ppermute(value, ("lon", "lat"), pairs)


def halo(info, turn, value, messages, shift, waits=()):
    sides = [swapped(messages[start], "lon", start, True) for start in (1, 0)]
    rows = jax.ShapeDtypeStruct((3 * SPAN, WIDTH), bf16)
    near, far, window, extra = run(
        rows_kernel,
        (rows, rows, rows, jax.ShapeDtypeStruct((4 * EDGE, WIDTH), bf16)),
        [
            pltpu.VMEM((WIDTH // LANES, ROWS, COLS + 16, LANES), f32),
            pltpu.VMEM((3, 3 * COLS, WIDTH), f32),
            pltpu.VMEM((6, SPAN, WIDTH), f32),
        ],
        (info, turn),
        value,
        *sides,
        waits=waits,
    )
    far = swapped(far, "lat", 1, False)
    near = swapped(near, "lat", 0, False)
    lat_count, lon_count = lax.axis_size("lat"), lax.axis_size("lon")
    moves = [fold_stage(FOLD * k, lat_count, lon_count) for k in range(lon_count // FOLD)]

    def branch(k, whole):
        return lambda window, extra: (moves[k](window), extra if whole else moves[k - 1](extra))

    branches = [branch(k, whole) for k in range(len(moves)) for whole in (True, False)]
    chosen = 2 * (shift // (FOLD * COLS)) + (turn[0] < BEYOND)
    return value, *sides, far, near, *lax.switch(chosen, branches, window, extra)


def layout():
    lat_count, lon_count = lax.axis_size("lat"), lax.axis_size("lon")
    high = 2 if lat_count > 2 else 1
    return (lon_count // ACROSS, ACROSS, lat_count // (2 * high), high, 2)


def device_groups():
    numbers = np.arange(math.prod(layout())).reshape(layout()).transpose(4, 2, 1, 3, 0)
    plane = math.prod(numbers.shape[:3])
    lines = numbers.reshape(plane, -1)
    return lines.T.tolist(), lines.tolist()


def spread(value, groups):
    return lax.all_to_all(value, ("lon", "lat"), 0, 0, axis_index_groups=groups, tiled=True)


def reordered(weights):
    split = weights.reshape(layout() + (-1, weights.shape[1]))
    return split.transpose(4, 2, 1, 3, 0, 5, 6).reshape(weights.shape)


def body(fields, cotangent, land_sea, partner, kernel, gain, w_in, w_out):
    shape = jax.ShapeDtypeStruct
    total_cols = COLS * lax.axis_size("lon")
    shift = (partner[0] + 3) % total_cols
    turn = (shift % (FOLD * COLS)).reshape(1)
    at_top = lax.axis_index("lat") == lax.axis_size("lat") - 1
    info = jnp.stack([at_top.astype(jnp.int32), lax.axis_index("lon") % 2, lax.axis_index("lat") % 2])
    grid_shape = shape((ROWS, COLS, WIDTH), bf16)
    side = shape((ROWS * EDGE + 3 * COLS, WIDTH), bf16)
    edge_shapes = (side, side)
    wide = pltpu.VMEM((WIDTH // LANES, ROWS + 6, COLS + 16, LANES), f32)
    grid = pltpu.VMEM((ROWS, COLS, WIDTH), f32)
    planes, lines = device_groups()
    plane, depth = len(planes[0]), len(lines[0])
    span = HIDDEN // plane
    weights = reordered(w_in), reordered(w_out)
    sent = run(edge_kernel, edge_shapes, [], (info,), fields)
    block_out, dconved, message0, message1, message = run(
        main_kernel,
        (grid_shape, grid_shape) + edge_shapes + (shape((plane, 4 * span + 16, LANES), bf16),),
        [wide, grid, pltpu.VMEM((plane, 8, LANES), f32)],
        (info, turn),
        *halo(info, turn, fields, sent, shift, weights),
        cotangent,
        land_sea,
        kernel,
        gain.reshape(1, WIDTH),
        *weights,
    )
    rims = halo(info, turn, dconved, (message0, message1), shift)
    message = run(
        plane_kernel,
        shape((depth, 4 * span // depth + 8, LANES), bf16),
        [pltpu.VMEM((4 * span, LANES), f32)],
        (),
        spread(message, planes),
        waits=rims[1:3],
    )
    factor = 1.0 / math.sqrt(CELLS * lax.axis_size("lat") * lax.axis_size("lon"))
    share = shape((span // depth, WIDTH), f32)
    grad_w_in, grad_w_out, message = run(
        functools.partial(depth_kernel, factor),
        (share, share, shape((plane, 8, LANES), f32)),
        [],
        (),
        spread(message, lines),
        waits=rims[3:],
    )
    grad_kernel, grad_gain = run(
        gather_kernel,
        (shape((7, 7, WIDTH), f32), shape((1, WIDTH), f32)),
        [],
        (),
        spread(message, planes),
    )
    grad_input = run(grad_input_kernel, grid_shape, [wide, grid], (info, turn), *rims, cotangent, land_sea, kernel)
    return block_out, grad_input, grad_w_in, grad_w_out, grad_kernel, grad_gain.reshape(WIDTH)


def solution(mesh):
    cells = P("lat", "lon", None)
    share = P(("lon", "lat"), None)
    return jax.shard_map(
        body,
        mesh=mesh,
        in_specs=(cells, cells, P("lat", "lon"), P(), P(), P(), P(), P()),
        out_specs=(cells, cells, share, share, P(), P()),
        check_vma=False,
    )
```

```python
import functools
import math

import jax
import jax.numpy as jnp
import numpy as np
from jax import lax
from jax.experimental import pallas as pl
from jax.experimental.pallas import tpu as pltpu
from jax.sharding import PartitionSpec as P

EPS = 1e-06
ROWS, COLS, WIDTH, HIDDEN = 8, 32, 256, 1024
CELLS = ROWS * COLS
LANES = 128
CHUNK = 256
LEFT = 8
ACROSS = 4
EDGE = 8
SPAN = COLS + EDGE
FOLD = 2
BEYOND = 5
GELU_A = math.sqrt(2.0 / math.pi)
GELU_B = 0.044715
f32, bf16 = jnp.float32, jnp.bfloat16


def dot(left, right, dims):
    return lax.dot_general(left, right, (dims, ((), ())), preferred_element_type=f32)


def put(wide, rows, columns, value):
    for half in range(WIDTH // LANES):
        wide[half, rows, columns, :] = value[..., half * LANES : half * LANES + LANES]


def edges(info, grid, messages):
    block = grid[ROWS - 3 :].reshape(3 * COLS, WIDTH).astype(bf16)
    left, right = [
        grid[:, start : start + EDGE].reshape(ROWS * EDGE, WIDTH).astype(bf16) for start in (0, COLS - EDGE)
    ]
    even = info[1] == 0
    for message, here, there in zip(messages, (right, left), (left, right)):
        message[pl.ds(0, ROWS * EDGE), :] = jnp.where(even, here.astype(f32), there.astype(f32)).astype(bf16)
        message[pl.ds(ROWS * EDGE, 3 * COLS), :] = block


def edge_kernel(info, own, *messages):
    edges(info, own[...].astype(f32), messages)


def middle(info, wide, first, own, sides):
    put(wide, pl.ds(first, ROWS), pl.ds(LEFT, COLS), own[...].astype(f32))
    margin = pl.ds(0, ROWS * EDGE)
    for parity, starts in enumerate(((LEFT + COLS, 0), (0, LEFT + COLS))):

        @pl.when(info[1] == parity)
        def _():
            for start, side in zip(starts, sides):
                part = side[margin, :].astype(f32).reshape(ROWS, EDGE, WIDTH)
                put(wide, pl.ds(first, ROWS), pl.ds(start, EDGE), part)


def rows_kernel(info, turn, own, side1, side0, *refs):
    near, far, window, extra, wide, line, strip = refs[-7:]
    middle(info, wide, 0, own, (side0, side1))
    columns = pl.ds(LEFT - 3, SPAN)
    for parity, order in enumerate(((near, far), (far, near))):

        @pl.when(info[2] == parity)
        def _():
            for message, start in zip(order, (ROWS - 3, 0)):
                for half in range(WIDTH // LANES):
                    part = wide[half, pl.ds(start, 3), columns, :].reshape(3 * SPAN, LANES)
                    message[:, pl.ds(half * LANES, LANES)] = part.astype(bf16)

    @pl.when(info[0] == 1)
    def _():
        block = pl.ds(ROWS * EDGE, 3 * COLS)
        line[:, pl.ds(COLS, COLS), :] = own[pl.ds(ROWS - 3, 3)].astype(f32)
        for parity, starts in enumerate(((2 * COLS, 0), (0, 2 * COLS))):

            @pl.when(info[1] == parity)
            def _():
                for start, side in zip(starts, (side0, side1)):
                    line[:, pl.ds(start, COLS), :] = side[block, :].astype(f32).reshape(3, COLS, WIDTH)

        for column in range(COLS + 6):
            source = jnp.maximum(COLS + turn[0] - column, 0)
            for row in range(3):
                strip[row, pl.ds(column, 1), :] = line[2 - row, pl.ds(source, 1), :]
            if column > COLS:
                source = jnp.minimum((FOLD + 1) * COLS + turn[0] - column, 3 * COLS - 1)
                for row in range(3):
                    strip[3 + row, pl.ds(column - COLS - 1, 1), :] = line[2 - row, pl.ds(source, 1), :]
        extra[pl.ds(0, 3 * EDGE), :] = strip[pl.ds(3, 3), pl.ds(0, EDGE), :].reshape(3 * EDGE, WIDTH).astype(bf16)
        window[...] = strip[pl.ds(0, 3), :, :].reshape(3 * SPAN, WIDTH).astype(bf16)


def assemble(info, turn, own, side1, side0, far, window, extra, near, wide):
    middle(info, wide, 3, own, (side0, side1))
    columns = pl.ds(LEFT - 3, SPAN)
    for parity, (below, above) in enumerate(((far, near), (near, far))):

        @pl.when(info[2] == parity)
        def _():
            for part, start in ((below, 0), (above, ROWS + 3)):
                put(wide, pl.ds(start, 3), columns, part[...].astype(f32).reshape(3, SPAN, WIDTH))

    @pl.when(info[0] == 1)
    def _():
        put(wide, pl.ds(ROWS + 3, 3), columns, window[...].astype(f32).reshape(3, SPAN, WIDTH))
        rest = extra[pl.ds(0, 3 * EDGE), :].astype(f32).reshape(3, EDGE, WIDTH)
        for place in range(BEYOND):
            column = COLS + 1 + place

            @pl.when(turn[0] - column < -COLS)
            def _():
                put(wide, pl.ds(ROWS + 3, 3), pl.ds(LEFT - 3 + column, 1), rest[:, place : place + 1])


def keepers(land):
    spot = lax.broadcasted_iota(jnp.int32, (1, COLS, COLS), 1) == lax.broadcasted_iota(jnp.int32, (1, COLS, COLS), 2)
    values = land[...].astype(f32)[:, None, :]
    return jnp.sum(jnp.where(spot, values, 0.0), -1, keepdims=True)


def main_kernel(
    info, turn, own, side1, side0, far, window, extra, near, cot, land, taps, gain, w_in, w_out,
    block_out, dconv, message0, message1, message, wide, grid, sums,
):
    assemble(info, turn, own, side1, side0, far, window, extra, near, wide)
    for half in range(WIDTH // LANES):
        lanes = pl.ds(half * LANES, LANES)
        for tile in range(COLS // 8):
            total = jnp.zeros((ROWS, 8, LANES), f32)
            for b in range(7):
                block = wide[half, :, pl.ds(LEFT - 3 + tile * 8 + b, 8), :]
                for a in range(7):
                    total = total + block[a : a + ROWS] * taps[a, pl.ds(b, 1), lanes][None]
            grid[:, pl.ds(tile * 8, 8), lanes] = total
    flat = grid[...].reshape(CELLS, WIDTH)
    average = jnp.mean(flat, -1, keepdims=True)
    centred = flat - average
    rstd = lax.rsqrt(jnp.mean(centred * centred, -1, keepdims=True) + EPS)
    normed = centred * rstd
    gains = gain[...]
    scaled = (normed * gains).astype(bf16)
    keeper = keepers(land)
    upstream = (keeper * cot[...].astype(f32)).astype(bf16).reshape(CELLS, WIDTH)
    branch = jnp.zeros((CELLS, WIDTH), f32)
    dscaled = jnp.zeros((CELLS, WIDTH), f32)
    plane, span = message.shape[0], HIDDEN // message.shape[0]
    for chunk in range(HIDDEN // CHUNK):
        units = pl.ds(chunk * CHUNK, CHUNK)
        w_in_part, w_out_part = w_in[units, :], w_out[units, :]
        before = dot(scaled, w_in_part, ((1,), (1,)))
        square = before * before
        bend = jnp.tanh(before * (GELU_A + (GELU_A * GELU_B) * square))
        gate = 0.5 + 0.5 * bend
        hidden = (before * gate).astype(bf16)
        slope = gate + (0.5 * before) * (1.0 - bend * bend) * (GELU_A + (3.0 * GELU_A * GELU_B) * square)
        branch = branch + dot(hidden, w_out_part, ((1,), (0,)))
        dbefore = (dot(upstream, w_out_part, ((1,), (1,))) * slope).astype(bf16)
        dscaled = dscaled + dot(dbefore, w_in_part, ((1,), (0,)))
        places = pl.ds(chunk * CHUNK // span, CHUNK // span)
        for pair, (units_of, cells_of) in enumerate(((dbefore, scaled), (hidden, upstream))):
            product = dot(units_of, cells_of, ((0,), (0,))).astype(bf16)
            for half in range(2):
                part = product[:, half * LANES : half * LANES + LANES]
                message[places, pl.ds((2 * pair + half) * span, span), :] = part.reshape(CHUNK // span, span, LANES)
    block_out[...] = (keeper * (own[...].astype(f32) + branch.reshape(ROWS, COLS, WIDTH))).astype(bf16)
    dnormed = dscaled * gains
    dconved = rstd * (
        dnormed - jnp.mean(dnormed, -1, keepdims=True) - normed * jnp.mean(dnormed * normed, -1, keepdims=True)
    )
    dconv[...] = dconved.astype(bf16).reshape(ROWS, COLS, WIDTH)
    grid[...] = dconved.reshape(ROWS, COLS, WIDTH)
    edges(info, grid[...], (message0, message1))
    gain_row = jnp.sum(dscaled * normed, 0, keepdims=True)
    sums[...] = jnp.zeros(sums.shape, f32)
    for half in range(WIDTH // LANES):
        lanes = pl.ds(half * LANES, LANES)
        sums[49 // 2, pl.ds(2 + half, 1), :] = gain_row[:, half * LANES : half * LANES + LANES]
        for b in range(7):
            totals = [jnp.zeros((8, LANES), f32) for _ in range(7)]
            for tile in range(COLS // 8):
                block = wide[half, :, pl.ds(LEFT - 3 + tile * 8 + b, 8), :]
                here = grid[:, pl.ds(tile * 8, 8), lanes]
                for a in range(7):
                    totals[a] = totals[a] + jnp.sum(block[a : a + ROWS] * here, 0)
            for a in range(7):
                tap = 7 * a + b
                sums[tap // 2, pl.ds(2 * (tap % 2) + half, 1), :] = jnp.sum(totals[a], 0, keepdims=True)
    message[:, pl.ds(4 * span, 16), :] = small_pack(sums[...]).astype(bf16)


def small_pack(sums):
    high = sums.astype(bf16).astype(f32)
    low = sums - high
    return jnp.concatenate([high[:, :4], low[:, :4], jnp.zeros_like(sums)], 1)


def grad_input_kernel(
    info, turn, own, side1, side0, far, window, extra, near, cot, land, taps, grad_input, wide, upstream
):
    assemble(info, turn, own, side1, side0, far, window, extra, near, wide)
    folded = info[0] == 1
    upstream[...] = keepers(land) * cot[...].astype(f32)
    for half in range(WIDTH // LANES):
        lanes = pl.ds(half * LANES, LANES)
        for tile in range(COLS // 8):
            total = upstream[:, pl.ds(tile * 8, 8), lanes]
            for b in range(7):
                block = wide[half, :, pl.ds(LEFT - 3 + tile * 8 + b, 8), :]
                for a in range(7):
                    weight = taps[6 - a, pl.ds(6 - b, 1), lanes][None]
                    if a > 3:
                        rim = jnp.where(folded, taps[a, pl.ds(b, 1), lanes][None], weight)
                        weight = jnp.concatenate(
                            [
                                jnp.broadcast_to(weight, (11 - a, 1, LANES)),
                                jnp.broadcast_to(rim, (a - 3, 1, LANES)),
                            ],
                            0,
                        )
                    total = total + block[a : a + ROWS] * weight
            grid_part = total.astype(bf16)
            grad_input[:, pl.ds(tile * 8, 8), lanes] = grid_part


def plane_kernel(received, *refs):
    message, total = refs[-2:]
    plane, lines = received.shape[0], received.shape[1] - 16
    depth = message.shape[0]
    each = lines // 4 // depth
    large = received[0, pl.ds(0, lines), :].astype(f32)
    small = received[0, pl.ds(lines, 16), :].astype(f32)
    for source in range(1, plane):
        large = large + received[source, pl.ds(0, lines), :].astype(f32)
        small = small + received[source, pl.ds(lines, 16), :].astype(f32)
    total[...] = large
    sums = small[:8]
    both = sums + jnp.concatenate([sums[4:], sums[:4]], 0)
    packed = small_pack(both[None])[0, :8]
    for place in range(depth):
        parts = [total[pl.ds(line * (lines // 4) + place * each, each), :] for line in range(4)]
        message[place] = jnp.concatenate(parts + [packed], 0).astype(bf16)


def depth_kernel(factor, received, *refs):
    first, second, message = refs[-3:]
    depth, lines = received.shape[0], received.shape[1] - 8
    total = received[0].astype(f32)
    for source in range(1, depth):
        total = total + received[source].astype(f32)
    total = total * factor
    each = lines // 4
    for half in range(2):
        lanes = pl.ds(half * LANES, LANES)
        first[:, lanes] = total[half * each : half * each + each]
        second[:, lanes] = total[(2 + half) * each : (3 + half) * each]
    sums = total[lines:]
    both = sums + jnp.concatenate([sums[4:], sums[:4]], 0)
    message[...] = jnp.broadcast_to(both[None], message.shape)


def gather_kernel(received, grad_kernel, grad_gain):
    for tap in range(50):
        for half in range(WIDTH // LANES):
            lanes = pl.ds(half * LANES, LANES)
            row = received[tap // 2, pl.ds(2 * (tap % 2) + half, 1), :]
            if tap == 49:
                grad_gain[:, lanes] = row
            else:
                grad_kernel[tap // 7, pl.ds(tap % 7, 1), lanes] = row


def run(kernel, out, scratch, scalars, *args, waits=()):
    whole = pl.BlockSpec(memory_space=pltpu.VMEM)
    specs = [pl.BlockSpec(memory_space=pltpu.SMEM)] * len(scalars) + [whole] * len(args)
    specs += [pl.BlockSpec(memory_space=pl.ANY)] * len(waits)
    call = pl.pallas_call(
        kernel,
        out_shape=out,
        in_specs=specs,
        out_specs=jax.tree.map(lambda _: whole, out),
        scratch_shapes=scratch,
        compiler_params=pltpu.CompilerParams(vmem_limit_bytes=48 * 1024 * 1024),
    )
    return call(*scalars, *args, *waits)


def swapped(value, axis, start, wrap):
    count = lax.axis_size(axis)
    pairs = [(i, (i + 1) % count) for i in range(start, count if wrap else count - 1, 2)]
    return lax.ppermute(value, axis, pairs + [(j, i) for i, j in pairs])


def fold_stage(step, lat_count, lon_count):
    pairs = [
        (((step - lon) % lon_count + 1) * lat_count - 1, (lon + 1) * lat_count - 1) for lon in range(lon_count)
    ]
    return lambda value: lax.ppermute(value, ("lon", "lat"), pairs)


def halo(info, turn, value, messages, shift, waits=()):
    sides = [swapped(messages[start], "lon", start, True) for start in (1, 0)]
    rows = jax.ShapeDtypeStruct((3 * SPAN, WIDTH), bf16)
    near, far, window, extra = run(
        rows_kernel,
        (rows, rows, rows, jax.ShapeDtypeStruct((4 * EDGE, WIDTH), bf16)),
        [
            pltpu.VMEM((WIDTH // LANES, ROWS, COLS + 16, LANES), f32),
            pltpu.VMEM((3, 3 * COLS, WIDTH), f32),
            pltpu.VMEM((6, SPAN, WIDTH), f32),
        ],
        (info, turn),
        value,
        *sides,
        waits=waits,
    )
    lat_count, lon_count = lax.axis_size("lat"), lax.axis_size("lon")
    moves = [fold_stage(FOLD * k, lat_count, lon_count) for k in range(lon_count // FOLD)]

    def branch(k, whole):
        def exchange(far, window, extra, near):
            far = swapped(far, "lat", 1, False)
            window = moves[k](window)
            extra = extra if whole else moves[k - 1](extra)
            return far, window, extra, swapped(near, "lat", 0, False)

        return exchange

    branches = [branch(k, whole) for k in range(len(moves)) for whole in (True, False)]
    chosen = 2 * (shift // (FOLD * COLS)) + (turn[0] < BEYOND)
    return value, *sides, *lax.switch(chosen, branches, far, window, extra, near)


def layout():
    lat_count, lon_count = lax.axis_size("lat"), lax.axis_size("lon")
    high = 2 if lat_count > 2 else 1
    return (lon_count // ACROSS, ACROSS, lat_count // (2 * high), high, 2)


def device_groups():
    numbers = np.arange(math.prod(layout())).reshape(layout()).transpose(4, 2, 1, 3, 0)
    plane = math.prod(numbers.shape[:3])
    lines = numbers.reshape(plane, -1)
    return lines.T.tolist(), lines.tolist()


def spread(value, groups):
    return lax.all_to_all(value, ("lon", "lat"), 0, 0, axis_index_groups=groups, tiled=True)


def reordered(weights):
    split = weights.reshape(layout() + (-1, weights.shape[1]))
    return split.transpose(4, 2, 1, 3, 0, 5, 6).reshape(weights.shape)


def body(fields, cotangent, land_sea, partner, kernel, gain, w_in, w_out):
    shape = jax.ShapeDtypeStruct
    total_cols = COLS * lax.axis_size("lon")
    shift = (partner[0] + 3) % total_cols
    turn = (shift % (FOLD * COLS)).reshape(1)
    at_top = lax.axis_index("lat") == lax.axis_size("lat") - 1
    info = jnp.stack([at_top.astype(jnp.int32), lax.axis_index("lon") % 2, lax.axis_index("lat") % 2])
    grid_shape = shape((ROWS, COLS, WIDTH), bf16)
    side = shape((ROWS * EDGE + 3 * COLS, WIDTH), bf16)
    edge_shapes = (side, side)
    wide = pltpu.VMEM((WIDTH // LANES, ROWS + 6, COLS + 16, LANES), f32)
    grid = pltpu.VMEM((ROWS, COLS, WIDTH), f32)
    planes, lines = device_groups()
    plane, depth = len(planes[0]), len(lines[0])
    span = HIDDEN // plane
    weights = reordered(w_in), reordered(w_out)
    sent = run(edge_kernel, edge_shapes, [], (info,), fields)
    block_out, dconved, message0, message1, message = run(
        main_kernel,
        (grid_shape, grid_shape) + edge_shapes + (shape((plane, 4 * span + 16, LANES), bf16),),
        [wide, grid, pltpu.VMEM((plane, 8, LANES), f32)],
        (info, turn),
        *halo(info, turn, fields, sent, shift, weights),
        cotangent,
        land_sea,
        kernel,
        gain.reshape(1, WIDTH),
        *weights,
    )
    rims = halo(info, turn, dconved, (message0, message1), shift)
    message = run(
        plane_kernel,
        shape((depth, 4 * span // depth + 8, LANES), bf16),
        [pltpu.VMEM((4 * span, LANES), f32)],
        (),
        spread(message, planes),
        waits=rims[1:3],
    )
    factor = 1.0 / math.sqrt(CELLS * lax.axis_size("lat") * lax.axis_size("lon"))
    share = shape((span // depth, WIDTH), f32)
    grad_w_in, grad_w_out, message = run(
        functools.partial(depth_kernel, factor),
        (share, share, shape((plane, 8, LANES), f32)),
        [],
        (),
        spread(message, lines),
        waits=rims[3:],
    )
    grad_kernel, grad_gain = run(
        gather_kernel,
        (shape((7, 7, WIDTH), f32), shape((1, WIDTH), f32)),
        [],
        (),
        spread(message, planes),
    )
    grad_input = run(grad_input_kernel, grid_shape, [wide, grid], (info, turn), *rims, cotangent, land_sea, kernel)
    return block_out, grad_input, grad_w_in, grad_w_out, grad_kernel, grad_gain.reshape(WIDTH)


def solution(mesh):
    cells = P("lat", "lon", None)
    share = P(("lon", "lat"), None)
    return jax.shard_map(
        body,
        mesh=mesh,
        in_specs=(cells, cells, P("lat", "lon"), P(), P(), P(), P(), P()),
        out_specs=(cells, cells, share, share, P(), P()),
        check_vma=False,
    )
```

```python
import functools
import math

import jax
import jax.numpy as jnp
import numpy as np
from jax import lax
from jax.experimental import pallas as pl
from jax.experimental.pallas import tpu as pltpu
from jax.sharding import PartitionSpec as P

EPS = 1e-06
ROWS, COLS, WIDTH, HIDDEN = 8, 32, 256, 1024
CELLS = ROWS * COLS
LANES = 128
CHUNK = 512
LEFT = 8
ACROSS = 4
EDGE = 8
SPAN = COLS + EDGE
FOLD = 2
BEYOND = 5
GELU_A = math.sqrt(2.0 / math.pi)
GELU_B = 0.044715
f32, bf16 = jnp.float32, jnp.bfloat16


def dot(left, right, dims):
    return lax.dot_general(left, right, (dims, ((), ())), preferred_element_type=f32)


def put(wide, rows, columns, value):
    for half in range(WIDTH // LANES):
        wide[half, rows, columns, :] = value[..., half * LANES : half * LANES + LANES]


def edges(info, grid, messages):
    block = grid[ROWS - 3 :].reshape(3 * COLS, WIDTH).astype(bf16)
    left, right = [
        grid[:, start : start + EDGE].reshape(ROWS * EDGE, WIDTH).astype(bf16) for start in (0, COLS - EDGE)
    ]
    even = info[1] == 0
    for message, here, there in zip(messages, (right, left), (left, right)):
        message[pl.ds(0, ROWS * EDGE), :] = jnp.where(even, here.astype(f32), there.astype(f32)).astype(bf16)
        message[pl.ds(ROWS * EDGE, 3 * COLS), :] = block


def edge_kernel(info, own, *messages):
    edges(info, own[...].astype(f32), messages)


def middle(info, wide, first, own, sides):
    put(wide, pl.ds(first, ROWS), pl.ds(LEFT, COLS), own[...].astype(f32))
    margin = pl.ds(0, ROWS * EDGE)
    for parity, starts in enumerate(((LEFT + COLS, 0), (0, LEFT + COLS))):

        @pl.when(info[1] == parity)
        def _():
            for start, side in zip(starts, sides):
                part = side[margin, :].astype(f32).reshape(ROWS, EDGE, WIDTH)
                put(wide, pl.ds(first, ROWS), pl.ds(start, EDGE), part)


def rows_kernel(info, turn, own, side1, side0, *refs):
    near, far, window, extra, wide, line, strip = refs[-7:]
    middle(info, wide, 0, own, (side0, side1))
    columns = pl.ds(LEFT - 3, SPAN)
    for parity, order in enumerate(((near, far), (far, near))):

        @pl.when(info[2] == parity)
        def _():
            for message, start in zip(order, (ROWS - 3, 0)):
                for half in range(WIDTH // LANES):
                    part = wide[half, pl.ds(start, 3), columns, :].reshape(3 * SPAN, LANES)
                    message[:, pl.ds(half * LANES, LANES)] = part.astype(bf16)

    @pl.when(info[0] == 1)
    def _():
        block = pl.ds(ROWS * EDGE, 3 * COLS)
        line[:, pl.ds(COLS, COLS), :] = own[pl.ds(ROWS - 3, 3)].astype(f32)
        for parity, starts in enumerate(((2 * COLS, 0), (0, 2 * COLS))):

            @pl.when(info[1] == parity)
            def _():
                for start, side in zip(starts, (side0, side1)):
                    line[:, pl.ds(start, COLS), :] = side[block, :].astype(f32).reshape(3, COLS, WIDTH)

        for column in range(COLS + 6):
            source = jnp.maximum(COLS + turn[0] - column, 0)
            for row in range(3):
                strip[row, pl.ds(column, 1), :] = line[2 - row, pl.ds(source, 1), :]
            if column > COLS:
                source = jnp.minimum((FOLD + 1) * COLS + turn[0] - column, 3 * COLS - 1)
                for row in range(3):
                    strip[3 + row, pl.ds(column - COLS - 1, 1), :] = line[2 - row, pl.ds(source, 1), :]
        extra[pl.ds(0, 3 * EDGE), :] = strip[pl.ds(3, 3), pl.ds(0, EDGE), :].reshape(3 * EDGE, WIDTH).astype(bf16)
        window[...] = strip[pl.ds(0, 3), :, :].reshape(3 * SPAN, WIDTH).astype(bf16)


def assemble(info, turn, own, side1, side0, far, window, extra, near, wide):
    middle(info, wide, 3, own, (side0, side1))
    columns = pl.ds(LEFT - 3, SPAN)
    for parity, (below, above) in enumerate(((far, near), (near, far))):

        @pl.when(info[2] == parity)
        def _():
            for part, start in ((below, 0), (above, ROWS + 3)):
                put(wide, pl.ds(start, 3), columns, part[...].astype(f32).reshape(3, SPAN, WIDTH))

    @pl.when(info[0] == 1)
    def _():
        put(wide, pl.ds(ROWS + 3, 3), columns, window[...].astype(f32).reshape(3, SPAN, WIDTH))
        rest = extra[pl.ds(0, 3 * EDGE), :].astype(f32).reshape(3, EDGE, WIDTH)
        for place in range(BEYOND):
            column = COLS + 1 + place

            @pl.when(turn[0] - column < -COLS)
            def _():
                put(wide, pl.ds(ROWS + 3, 3), pl.ds(LEFT - 3 + column, 1), rest[:, place : place + 1])


def keepers(land):
    spot = lax.broadcasted_iota(jnp.int32, (1, COLS, COLS), 1) == lax.broadcasted_iota(jnp.int32, (1, COLS, COLS), 2)
    values = land[...].astype(f32)[:, None, :]
    return jnp.sum(jnp.where(spot, values, 0.0), -1, keepdims=True)


def main_kernel(
    info, turn, own, side1, side0, far, window, extra, near, cot, land, taps, gain, w_in, w_out,
    block_out, dconv, message0, message1, message, wide, grid, sums,
):
    assemble(info, turn, own, side1, side0, far, window, extra, near, wide)
    for half in range(WIDTH // LANES):
        lanes = pl.ds(half * LANES, LANES)
        for tile in range(COLS // 8):
            total = jnp.zeros((ROWS, 8, LANES), f32)
            for b in range(7):
                block = wide[half, :, pl.ds(LEFT - 3 + tile * 8 + b, 8), :]
                for a in range(7):
                    total = total + block[a : a + ROWS] * taps[a, pl.ds(b, 1), lanes][None]
            grid[:, pl.ds(tile * 8, 8), lanes] = total
    flat = grid[...].reshape(CELLS, WIDTH)
    average = jnp.mean(flat, -1, keepdims=True)
    centred = flat - average
    rstd = lax.rsqrt(jnp.mean(centred * centred, -1, keepdims=True) + EPS)
    normed = centred * rstd
    gains = gain[...]
    scaled = (normed * gains).astype(bf16)
    keeper = keepers(land)
    upstream = (keeper * cot[...].astype(f32)).astype(bf16).reshape(CELLS, WIDTH)
    branch = jnp.zeros((CELLS, WIDTH), f32)
    dscaled = jnp.zeros((CELLS, WIDTH), f32)
    plane, span = message.shape[0], HIDDEN // message.shape[0]
    for chunk in range(HIDDEN // CHUNK):
        units = pl.ds(chunk * CHUNK, CHUNK)
        w_in_part, w_out_part = w_in[units, :], w_out[units, :]
        before = dot(scaled, w_in_part, ((1,), (1,)))
        square = before * before
        bend = jnp.tanh(before * (GELU_A + (GELU_A * GELU_B) * square))
        gate = 0.5 + 0.5 * bend
        hidden = (before * gate).astype(bf16)
        slope = gate + (0.5 * before) * (1.0 - bend * bend) * (GELU_A + (3.0 * GELU_A * GELU_B) * square)
        branch = branch + dot(hidden, w_out_part, ((1,), (0,)))
        dbefore = (dot(upstream, w_out_part, ((1,), (1,))) * slope).astype(bf16)
        dscaled = dscaled + dot(dbefore, w_in_part, ((1,), (0,)))
        places = pl.ds(chunk * CHUNK // span, CHUNK // span)
        for pair, (units_of, cells_of) in enumerate(((dbefore, scaled), (hidden, upstream))):
            product = dot(units_of, cells_of, ((0,), (0,))).astype(bf16)
            for half in range(2):
                part = product[:, half * LANES : half * LANES + LANES]
                message[places, pl.ds((2 * pair + half) * span, span), :] = part.reshape(CHUNK // span, span, LANES)
    block_out[...] = (keeper * (own[...].astype(f32) + branch.reshape(ROWS, COLS, WIDTH))).astype(bf16)
    dnormed = dscaled * gains
    dconved = rstd * (
        dnormed - jnp.mean(dnormed, -1, keepdims=True) - normed * jnp.mean(dnormed * normed, -1, keepdims=True)
    )
    dconv[...] = dconved.astype(bf16).reshape(ROWS, COLS, WIDTH)
    grid[...] = dconved.reshape(ROWS, COLS, WIDTH)
    edges(info, grid[...], (message0, message1))
    gain_row = jnp.sum(dscaled * normed, 0, keepdims=True)
    sums[...] = jnp.zeros(sums.shape, f32)
    for half in range(WIDTH // LANES):
        lanes = pl.ds(half * LANES, LANES)
        sums[49 // 2, pl.ds(2 + half, 1), :] = gain_row[:, half * LANES : half * LANES + LANES]
        for b in range(7):
            totals = [jnp.zeros((8, LANES), f32) for _ in range(7)]
            for tile in range(COLS // 8):
                block = wide[half, :, pl.ds(LEFT - 3 + tile * 8 + b, 8), :]
                here = grid[:, pl.ds(tile * 8, 8), lanes]
                for a in range(7):
                    for row in range(ROWS):
                        totals[a] = totals[a] + block[a + row] * here[row]
            for a in range(7):
                tap = 7 * a + b
                sums[tap // 2, pl.ds(2 * (tap % 2) + half, 1), :] = jnp.sum(totals[a], 0, keepdims=True)
    message[:, pl.ds(4 * span, 16), :] = small_pack(sums[...]).astype(bf16)


def small_pack(sums):
    high = sums.astype(bf16).astype(f32)
    low = sums - high
    return jnp.concatenate([high[:, :4], low[:, :4], jnp.zeros_like(sums)], 1)


def grad_input_kernel(
    info, turn, own, side1, side0, far, window, extra, near, cot, land, taps, grad_input, wide, upstream
):
    assemble(info, turn, own, side1, side0, far, window, extra, near, wide)
    folded = info[0] == 1
    upstream[...] = keepers(land) * cot[...].astype(f32)
    for half in range(WIDTH // LANES):
        lanes = pl.ds(half * LANES, LANES)
        for tile in range(COLS // 8):
            total = upstream[:, pl.ds(tile * 8, 8), lanes]
            for b in range(7):
                block = wide[half, :, pl.ds(LEFT - 3 + tile * 8 + b, 8), :]
                for a in range(7):
                    weight = taps[6 - a, pl.ds(6 - b, 1), lanes][None]
                    if a > 3:
                        rim = jnp.where(folded, taps[a, pl.ds(b, 1), lanes][None], weight)
                        weight = jnp.concatenate(
                            [
                                jnp.broadcast_to(weight, (11 - a, 1, LANES)),
                                jnp.broadcast_to(rim, (a - 3, 1, LANES)),
                            ],
                            0,
                        )
                    total = total + block[a : a + ROWS] * weight
            grid_part = total.astype(bf16)
            grad_input[:, pl.ds(tile * 8, 8), lanes] = grid_part


def plane_kernel(received, *refs):
    message, total = refs[-2:]
    plane, lines = received.shape[0], received.shape[1] - 16
    depth = message.shape[0]
    each = lines // 4 // depth
    large = received[0, pl.ds(0, lines), :].astype(f32)
    small = received[0, pl.ds(lines, 16), :].astype(f32)
    for source in range(1, plane):
        large = large + received[source, pl.ds(0, lines), :].astype(f32)
        small = small + received[source, pl.ds(lines, 16), :].astype(f32)
    total[...] = large
    sums = small[:8]
    both = sums + jnp.concatenate([sums[4:], sums[:4]], 0)
    packed = small_pack(both[None])[0, :8]
    for place in range(depth):
        parts = [total[pl.ds(line * (lines // 4) + place * each, each), :] for line in range(4)]
        message[place] = jnp.concatenate(parts + [packed], 0).astype(bf16)


def depth_kernel(factor, received, *refs):
    first, second, message = refs[-3:]
    depth, lines = received.shape[0], received.shape[1] - 8
    total = received[0].astype(f32)
    for source in range(1, depth):
        total = total + received[source].astype(f32)
    total = total * factor
    each = lines // 4
    for half in range(2):
        lanes = pl.ds(half * LANES, LANES)
        first[:, lanes] = total[half * each : half * each + each]
        second[:, lanes] = total[(2 + half) * each : (3 + half) * each]
    sums = total[lines:]
    both = sums + jnp.concatenate([sums[4:], sums[:4]], 0)
    message[...] = jnp.broadcast_to(both[None], message.shape)


def gather_kernel(received, grad_kernel, grad_gain):
    for tap in range(50):
        for half in range(WIDTH // LANES):
            lanes = pl.ds(half * LANES, LANES)
            row = received[tap // 2, pl.ds(2 * (tap % 2) + half, 1), :]
            if tap == 49:
                grad_gain[:, lanes] = row
            else:
                grad_kernel[tap // 7, pl.ds(tap % 7, 1), lanes] = row


def run(kernel, out, scratch, scalars, *args, waits=()):
    whole = pl.BlockSpec(memory_space=pltpu.VMEM)
    specs = [pl.BlockSpec(memory_space=pltpu.SMEM)] * len(scalars) + [whole] * len(args)
    specs += [pl.BlockSpec(memory_space=pl.ANY)] * len(waits)
    call = pl.pallas_call(
        kernel,
        out_shape=out,
        in_specs=specs,
        out_specs=jax.tree.map(lambda _: whole, out),
        scratch_shapes=scratch,
        compiler_params=pltpu.CompilerParams(vmem_limit_bytes=48 * 1024 * 1024),
    )
    return call(*scalars, *args, *waits)


def swapped(value, axis, start, wrap):
    count = lax.axis_size(axis)
    pairs = [(i, (i + 1) % count) for i in range(start, count if wrap else count - 1, 2)]
    return lax.ppermute(value, axis, pairs + [(j, i) for i, j in pairs])


def fold_stage(step, lat_count, lon_count):
    pairs = [
        (((step - lon) % lon_count + 1) * lat_count - 1, (lon + 1) * lat_count - 1) for lon in range(lon_count)
    ]
    return lambda value: lax.ppermute(value, ("lon", "lat"), pairs)


def halo(info, turn, value, messages, shift, waits=()):
    sides = [swapped(messages[start], "lon", start, True) for start in (1, 0)]
    rows = jax.ShapeDtypeStruct((3 * SPAN, WIDTH), bf16)
    near, far, window, extra = run(
        rows_kernel,
        (rows, rows, rows, jax.ShapeDtypeStruct((4 * EDGE, WIDTH), bf16)),
        [
            pltpu.VMEM((WIDTH // LANES, ROWS, COLS + 16, LANES), f32),
            pltpu.VMEM((3, 3 * COLS, WIDTH), f32),
            pltpu.VMEM((6, SPAN, WIDTH), f32),
        ],
        (info, turn),
        value,
        *sides,
        waits=waits,
    )
    lat_count, lon_count = lax.axis_size("lat"), lax.axis_size("lon")
    moves = [fold_stage(FOLD * k, lat_count, lon_count) for k in range(lon_count // FOLD)]

    def branch(k, whole):
        def exchange(far, window, extra, near):
            far = swapped(far, "lat", 1, False)
            window = moves[k](window)
            extra = extra if whole else moves[k - 1](extra)
            return far, window, extra, swapped(near, "lat", 0, False)

        return exchange

    branches = [branch(k, whole) for k in range(len(moves)) for whole in (True, False)]
    chosen = 2 * (shift // (FOLD * COLS)) + (turn[0] < BEYOND)
    return value, *sides, *lax.switch(chosen, branches, far, window, extra, near)


def layout():
    lat_count, lon_count = lax.axis_size("lat"), lax.axis_size("lon")
    high = 2 if lat_count > 2 else 1
    return (lon_count // ACROSS, ACROSS, lat_count // (2 * high), high, 2)


def device_groups():
    numbers = np.arange(math.prod(layout())).reshape(layout()).transpose(4, 2, 1, 3, 0)
    plane = math.prod(numbers.shape[:3])
    lines = numbers.reshape(plane, -1)
    return lines.T.tolist(), lines.tolist()


def spread(value, groups):
    return lax.all_to_all(value, ("lon", "lat"), 0, 0, axis_index_groups=groups, tiled=True)


def reordered(weights):
    split = weights.reshape(layout() + (-1, weights.shape[1]))
    return split.transpose(4, 2, 1, 3, 0, 5, 6).reshape(weights.shape)


def body(fields, cotangent, land_sea, partner, kernel, gain, w_in, w_out):
    shape = jax.ShapeDtypeStruct
    total_cols = COLS * lax.axis_size("lon")
    shift = (partner[0] + 3) % total_cols
    turn = (shift % (FOLD * COLS)).reshape(1)
    at_top = lax.axis_index("lat") == lax.axis_size("lat") - 1
    info = jnp.stack([at_top.astype(jnp.int32), lax.axis_index("lon") % 2, lax.axis_index("lat") % 2])
    grid_shape = shape((ROWS, COLS, WIDTH), bf16)
    side = shape((ROWS * EDGE + 3 * COLS, WIDTH), bf16)
    edge_shapes = (side, side)
    wide = pltpu.VMEM((WIDTH // LANES, ROWS + 6, COLS + 16, LANES), f32)
    grid = pltpu.VMEM((ROWS, COLS, WIDTH), f32)
    planes, lines = device_groups()
    plane, depth = len(planes[0]), len(lines[0])
    span = HIDDEN // plane
    weights = reordered(w_in), reordered(w_out)
    sent = run(edge_kernel, edge_shapes, [], (info,), fields)
    block_out, dconved, message0, message1, message = run(
        main_kernel,
        (grid_shape, grid_shape) + edge_shapes + (shape((plane, 4 * span + 16, LANES), bf16),),
        [wide, grid, pltpu.VMEM((plane, 8, LANES), f32)],
        (info, turn),
        *halo(info, turn, fields, sent, shift, weights),
        cotangent,
        land_sea,
        kernel,
        gain.reshape(1, WIDTH),
        *weights,
    )
    rims = halo(info, turn, dconved, (message0, message1), shift)
    message = run(
        plane_kernel,
        shape((depth, 4 * span // depth + 8, LANES), bf16),
        [pltpu.VMEM((4 * span, LANES), f32)],
        (),
        spread(message, planes),
        waits=rims[1:3],
    )
    factor = 1.0 / math.sqrt(CELLS * lax.axis_size("lat") * lax.axis_size("lon"))
    share = shape((span // depth, WIDTH), f32)
    grad_w_in, grad_w_out, message = run(
        functools.partial(depth_kernel, factor),
        (share, share, shape((plane, 8, LANES), f32)),
        [],
        (),
        spread(message, lines),
        waits=rims[3:],
    )
    grad_kernel, grad_gain = run(
        gather_kernel,
        (shape((7, 7, WIDTH), f32), shape((1, WIDTH), f32)),
        [],
        (),
        spread(message, planes),
    )
    grad_input = run(grad_input_kernel, grid_shape, [wide, grid], (info, turn), *rims, cotangent, land_sea, kernel)
    return block_out, grad_input, grad_w_in, grad_w_out, grad_kernel, grad_gain.reshape(WIDTH)


def solution(mesh):
    cells = P("lat", "lon", None)
    share = P(("lon", "lat"), None)
    return jax.shard_map(
        body,
        mesh=mesh,
        in_specs=(cells, cells, P("lat", "lon"), P(), P(), P(), P(), P()),
        out_specs=(cells, cells, share, share, P(), P()),
        check_vma=False,
    )
```
